32 devices in a mesh: cases: 2 (over y), gx: 16 (over z, x, core).
Axes of the slice: x: 2, y: 2, z: 4, core: 2. Of those that a mesh axis runs over, the one named last changes fastest.
Arguments:
- level_set: float32 [128, 256, 256], P(('cases', 'gx')), parts along dimension 0, may hold values from -6 to 6
- sensitivity: float32 [128, 256, 256], P(('cases', 'gx')), parts along dimension 0, may hold values from -2 to 2
- band: int32 [128, 256, 256], P(('cases', 'gx')), parts along dimension 0, may hold values 0 or 1
Outputs:
- speed: float32 [128, 256, 256], P(('cases', 'gx')), parts along dimension 0
- updated: float32 [128, 256, 256], P(('cases', 'gx')), parts along dimension 0
The draws below stay inside these ranges and needn't reach their ends.
There are 2 independent parts, one for each index of `cases`. The reference program is written for one: setup_inputs(seed, part) draws one part's arguments, and reference() takes and returns one part's arrays. A program takes and returns all parts, laid end to end along the dimension named above; each array names one. Nothing has to cross between parts.
All inputs are finite; a program needn't handle non-finite values. No bound on the sum of `band` on one device may be relied on, other than what follows from the above.
Results may differ from the reference program's by a relative error of at most 0.0003.
Values sent between devices are 32-bit elements; how exact they have to be, the bound alone decides.
No kernel may reach another device: no remote copies, remote signals or barrier semaphores. Data moves between devices by JAX's collectives and lax.ppermute only.
A program may use at most 64 MiB of HBM per device.

```python
import jax
import jax.numpy as jnp
from jax import lax

NY = 256
NZ = 256
SWEEPS = 4
REINIT = 2
NX = 64


def plant(entries, rng, smallest, high):
    place = [jax.random.randint(jax.random.fold_in(rng, axis), (), 0, length) for axis, length in enumerate(entries.shape)]
    main_axis = entries.shape.index(max(entries.shape))
    next_to = place[:main_axis] + [(place[main_axis] + 1) % entries.shape[main_axis]] + place[main_axis + 1:]
    return entries.at[tuple(place)].set(smallest).at[tuple(next_to)].set(high)


def block_scale(own_key, extent, cuts, least, high):
    factor_of = 1.0
    for position, blocks in cuts:
        steps = jax.random.uniform(jax.random.fold_in(jax.random.fold_in(own_key, 6), position), (blocks,), jnp.float32, least / len(cuts), high / len(cuts))
        factor_of = factor_of * jnp.repeat(jnp.exp(steps), extent[position] // blocks).reshape((-1,) + (1,) * (len(extent) - 1 - position))
    return factor_of


def normal_values(key, dims, scale, limit, pieces=(), held_as=jnp.bfloat16):
    level = block_scale(key, dims, pieces, -0.22, 0.18) if pieces else 1.0
    array = jax.random.normal(key, dims, jnp.float32) * scale * level
    return jnp.minimum(jnp.maximum(array, -limit), limit).astype(held_as)


def setup_inputs(seed: int = 0, part: int = 0) -> dict:
    arg_keys = jax.random.split(jax.random.key(seed), 4)
    part_splits = jax.random.split(jax.random.fold_in(arg_keys[3], part), 4)
    return {
        "level_set": normal_values(part_splits[0], (NX, NY, NZ), 1.0, 6.0, ((0, 16),), jnp.float32),
        "sensitivity": normal_values(part_splits[1], (NX, NY, NZ), 0.5, 2.0, ((0, 16),), jnp.float32),
        "band": plant((jax.random.randint(part_splits[2], (NX, NY, NZ), 0, 3) < 1).astype(jnp.int32), jax.random.fold_in(part_splits[2], 1), 0, 1),
    }


weno_eps = 1e-06
advect_step = 0.15
reinit_step = 0.3

def weno_blend(first, second, third, fourth, fifth):
    smooth_one = 13.0 / 12.0 * (first - 2.0 * second + third) ** 2 + 0.25 * (first - 4.0 * second + 3.0 * third) ** 2
    smooth_two = 13.0 / 12.0 * (second - 2.0 * third + fourth) ** 2 + 0.25 * (second - fourth) ** 2
    smooth_three = 13.0 / 12.0 * (third - 2.0 * fourth + fifth) ** 2 + 0.25 * (3.0 * third - 4.0 * fourth + fifth) ** 2
    alpha_one = 0.1 / (weno_eps + smooth_one) ** 2
    alpha_two = 0.6 / (weno_eps + smooth_two) ** 2
    alpha_three = 0.3 / (weno_eps + smooth_three) ** 2
    total = alpha_one + alpha_two + alpha_three
    blended = alpha_one * (first / 3.0 - 7.0 * second / 6.0 + 11.0 * third / 6.0)
    blended = blended + alpha_two * (-second / 6.0 + 5.0 * third / 6.0 + fourth / 3.0)
    blended = blended + alpha_three * (third / 3.0 + 5.0 * fourth / 6.0 - fifth / 6.0)
    return blended / total

def one_sided(shifted):
    diffs = [shifted[index + 1] - shifted[index] for index in range(6)]
    minus_side = weno_blend(diffs[0], diffs[1], diffs[2], diffs[3], diffs[4])
    plus_side = weno_blend(diffs[5], diffs[4], diffs[3], diffs[2], diffs[1])
    return (minus_side, plus_side)

def hamiltonian(padded, velocity):
    length = padded.shape[0]
    center = padded[3:length - 3]
    along_x = [lax.slice_in_dim(padded, 3 + offset, length - 3 + offset, axis=0) for offset in range(-3, 4)]
    walled = jnp.pad(center, ((0, 0), (3, 3), (0, 0)), mode='edge')
    width_y = center.shape[1]
    along_y = [lax.slice_in_dim(walled, 3 + offset, width_y + 3 + offset, axis=1) for offset in range(-3, 4)]
    along_z = [jnp.roll(center, -offset, axis=2) for offset in range(-3, 4)]
    positive = velocity > 0.0
    total = jnp.zeros_like(center)
    for shifted in (along_x, along_y, along_z):
        minus_side, plus_side = one_sided(shifted)
        rising = jnp.maximum(jnp.maximum(minus_side, 0.0) ** 2, jnp.minimum(plus_side, 0.0) ** 2)
        falling = jnp.maximum(jnp.minimum(minus_side, 0.0) ** 2, jnp.maximum(plus_side, 0.0) ** 2)
        total = total + jnp.where(positive, rising, falling)
    return jnp.sqrt(total)

def neighbour_mean(padded_x, field):
    length = padded_x.shape[0]
    walled = jnp.pad(field, ((0, 0), (1, 1), (0, 0)), mode='edge')
    total = padded_x[2:] + padded_x[:length - 2]
    total = total + walled[:, 2:] + walled[:, :-2]
    total = total + jnp.roll(field, -1, axis=2) + jnp.roll(field, 1, axis=2)
    return total / 6.0

def wrap_x(field, width):
    return jnp.pad(field, ((width, width), (0, 0), (0, 0)), mode='wrap')

def reference(level_set, sensitivity, band):
    weight = band.astype(jnp.float32)
    fixed = weight * sensitivity
    speed = fixed
    for sweep in range(SWEEPS):
        speed = weight * fixed + (1.0 - weight) * neighbour_mean(wrap_x(speed, 1), speed)

    def advect_rate(field):
        return -speed * hamiltonian(wrap_x(field, 3), speed)
    first = level_set + advect_step * advect_rate(level_set)
    second = 0.75 * level_set + 0.25 * (first + advect_step * advect_rate(first))
    advected = level_set / 3.0 + 2.0 / 3.0 * (second + advect_step * advect_rate(second))
    sign_field = advected / jnp.sqrt(advected * advected + 1.0)
    updated = advected
    for step in range(REINIT):
        updated = updated - reinit_step * sign_field * (hamiltonian(wrap_x(updated, 3), sign_field) - 1.0)
    return (speed, updated)
```

```python
import functools

import jax
import jax.numpy as jnp
from jax import lax
from jax.experimental import pallas as pl
from jax.experimental.pallas import tpu as pltpu
from jax.sharding import PartitionSpec as P

SWEEPS = 4
REINIT = 2
SUB = 8
CHUNKS = 2

weno_eps = 1e-06
advect_step = 0.15
reinit_step = 0.3


def recip(value):
    return pl.reciprocal(value, approx=True)


def face_pair(d, q6, s4, a, b, c, r_here, r_next):
    ratio_a = b * recip(a)
    ratio_c = b * recip(c)
    gain_a = ratio_a * ratio_a
    gain_c = ratio_c * ratio_c
    part_a = gain_a * r_here
    part_c = gain_c * r_next
    half = 0.5 * (gain_a + gain_c) + 3.0
    mid = d + 0.5 * q6
    minus = (mid + s4) - (part_a + 1.5 * part_c) * recip(half + gain_c)
    negated_plus = (s4 - mid) - (1.5 * part_a + part_c) * recip(half + gain_a)
    return minus, negated_plus


def smoothness(x, y, x_square, y_square):
    cross = x * y
    base = (x_square + y_square) + 0.75 * weno_eps
    outer = base - 2.75 * cross
    return outer + 1.5 * y_square, base - 1.25 * cross, outer + 1.5 * x_square


def along_line(cells):
    count = len(cells) - 6
    d = [cells[i + 1] - cells[i] for i in range(count + 5)]
    e = [d[i + 1] - d[i] for i in range(count + 4)]
    squares = [v * v for v in e]
    triples = [smoothness(e[i], e[i + 1], squares[i], squares[i + 1]) for i in range(count + 3)]
    q6 = [(e[i + 1] - e[i]) * (1.0 / 6.0) for i in range(count + 3)]
    r6 = [q6[i + 1] - q6[i] for i in range(count + 2)]
    faces = []
    for k in range(count + 1):
        s4 = 0.25 * (e[k + 1] + e[k + 2])
        faces.append(
            face_pair(
                d[k + 2], q6[k + 1], s4, triples[k][0], triples[k + 1][1], triples[k + 2][2], r6[k], r6[k + 1]
            )
        )
    return [(faces[i][0], faces[i + 1][1]) for i in range(count)]


def along_lanes(cell):
    length = cell.shape[1]

    def back(v):
        return pltpu.roll(v, 1, 1)

    def ahead(v):
        return pltpu.roll(v, length - 1, 1)

    d = ahead(cell) - cell
    x = d - back(d)
    y = ahead(x)
    a, b, c = smoothness(x, y, x * x, y * y)
    q6 = (y - x) * (1.0 / 6.0)
    r6 = q6 - back(q6)
    minus, negated_plus = face_pair(d, q6, 0.25 * (x + y), back(a), b, ahead(c), r6, ahead(r6))
    return back(minus), negated_plus


def upwind(pair, positive):
    minus, negated_plus = pair
    rising = jnp.maximum(jnp.maximum(minus, negated_plus), 0.0)
    falling = jnp.minimum(jnp.minimum(minus, negated_plus), 0.0)
    chosen = jnp.where(positive, rising, falling)
    return chosen * chosen


def upwind_both(pair):
    minus, negated_plus = pair
    rising = jnp.maximum(jnp.maximum(minus, negated_plus), 0.0)
    falling = jnp.minimum(jnp.minimum(minus, negated_plus), 0.0)
    return rising * rising, falling * falling


def shift_rows(tile, down):
    rows = lax.broadcasted_iota(jnp.int32, tile.shape, 0)
    if down:
        return jnp.where(rows == 0, tile, pltpu.roll(tile, 1, 0))
    return jnp.where(rows == SUB - 1, tile, pltpu.roll(tile, SUB - 1, 0))


def edge_tile(wrapped, nearest_row_tile, low):
    rows = lax.broadcasted_iota(jnp.int32, wrapped.shape, 0)
    if low:
        return jnp.where(rows == 0, nearest_row_tile, pltpu.roll(wrapped, 1, 0))
    return jnp.where(rows == SUB - 1, nearest_row_tile, pltpu.roll(wrapped, SUB - 1, 0))


def local_body(chunks, both, block, *refs):
    u_refs = refs[:chunks]
    if both:
        rise_ref, fall_ref, padded = refs[chunks:]
    else:
        vel_ref, out_ref, padded = refs[chunks:]
    tiles = padded.shape[0] - 6
    per = tiles // chunks
    for index in range(chunks):
        padded[3 + index * per : 3 + (index + 1) * per] = u_refs[index][0]
    first = padded[3]
    final = padded[tiles + 2]
    for step in range(3):
        padded[step] = edge_tile(padded[tiles + step], first, True)
        padded[tiles + 3 + step] = edge_tile(padded[3 + step], final, False)

    def loop(number, carry):
        start = number * block
        cells = [padded[start + i] for i in range(block + 6)]
        pairs = along_line(cells)
        for i in range(block):
            lanes = along_lanes(cells[i + 3])
            if both:
                rise_y, fall_y = upwind_both(pairs[i])
                rise_z, fall_z = upwind_both(lanes)
                rise_ref[0, start + i] = rise_y + rise_z
                fall_ref[0, start + i] = fall_y + fall_z
            else:
                positive = vel_ref[0, start + i] > 0.0
                out_ref[0, start + i] = upwind(pairs[i], positive) + upwind(lanes, positive)
        return carry

    lax.fori_loop(0, tiles // block, loop, 0)


def local_part(pieces, velocity, block=4):
    layers, per, _, lanes = pieces[0].shape
    tiles = per * len(pieces)
    both = velocity is None
    whole = pl.BlockSpec((1, tiles, SUB, lanes), lambda i: (i, 0, 0, 0))
    piece = pl.BlockSpec((1, per, SUB, lanes), lambda i: (i, 0, 0, 0))
    shape = jax.ShapeDtypeStruct((layers, tiles, SUB, lanes), jnp.float32)
    cells = layers * tiles * SUB * lanes
    return pl.pallas_call(
        functools.partial(local_body, len(pieces), both, block),
        grid=(layers,),
        in_specs=[piece] * len(pieces) + ([] if both else [whole]),
        out_specs=(whole, whole) if both else whole,
        out_shape=(shape, shape) if both else shape,
        scratch_shapes=[pltpu.VMEM((tiles + 6, SUB, lanes), jnp.float32)],
        compiler_params=pltpu.CompilerParams(vmem_limit_bytes=24 * 1024 * 1024),
        cost_estimate=pl.CostEstimate(flops=130 * cells, bytes_accessed=12 * cells, transcendentals=8 * cells),
        name="local_part",
    )(*pieces, *(() if both else (velocity,)))


def finish_body(kind, last, *refs):
    u_ref, left_ref, right_ref = refs[:3]
    rest = list(refs[3:])
    layers, tiles = u_ref.shape[0], u_ref.shape[1]
    if kind == "first":
        rise_ref, fall_ref, vel_ref = rest[:3]
        rest = rest[3:]
    else:
        local_ref, vel_ref = rest[:2]
        rest = rest[2:]
        if kind in ("second", "third"):
            base_ref = rest.pop(0)
    out_ref = rest[0]

    def loop(t, carry):
        own = [u_ref[i, t] for i in range(layers)]
        cells = [left_ref[i, t] for i in range(3)] + own + [right_ref[i, t] for i in range(3)]
        pairs = along_line(cells)
        for i in range(layers):
            vel = vel_ref[i, t]
            positive = vel > 0.0
            total = upwind(pairs[i], positive)
            if kind == "first":
                total = total + jnp.where(positive, rise_ref[i, t], fall_ref[i, t])
            else:
                total = total + local_ref[i, t]
            height = jnp.sqrt(total)
            if kind == "first":
                new = own[i] - advect_step * (vel * height)
            elif kind == "second":
                new = 0.75 * base_ref[i, t] + 0.25 * (own[i] - advect_step * (vel * height))
            elif kind == "third":
                new = base_ref[i, t] * (1.0 / 3.0) + (2.0 / 3.0) * (own[i] - advect_step * (vel * height))
            else:
                sign = vel * lax.rsqrt(vel * vel + 1.0)
                new = own[i] - reinit_step * (sign * (height - 1.0))
            out_ref[i, t] = new
            if not last:
                if i < 3:
                    rest[1][i, t] = new
                if i >= layers - 3:
                    rest[2][i - (layers - 3), t] = new
        return carry

    lax.fori_loop(0, tiles, loop, 0)


def finish_part(kind, last, index, u, left, right, others, block=4):
    layers, per, _, lanes = u.shape
    block = min(block, per)
    shift = index * (per // block)
    own = pl.BlockSpec((layers, block, SUB, lanes), lambda i: (0, i, 0, 0))
    side = pl.BlockSpec((3, block, SUB, lanes), lambda i: (0, i, 0, 0))
    moved = pl.BlockSpec((layers, block, SUB, lanes), lambda i: (0, i + shift, 0, 0))
    shape = jax.ShapeDtypeStruct(u.shape, jnp.float32)
    side_shape = jax.ShapeDtypeStruct((3, per, SUB, lanes), jnp.float32)
    specs = [moved if other.shape[1] != per else own for other in others]
    cells = layers * per * SUB * lanes
    return pl.pallas_call(
        functools.partial(finish_body, kind, last),
        grid=(per // block,),
        in_specs=[own, side, side] + specs,
        out_specs=own if last else (own, side, side),
        out_shape=shape if last else (shape, side_shape, side_shape),
        compiler_params=pltpu.CompilerParams(vmem_limit_bytes=24 * 1024 * 1024),
        cost_estimate=pl.CostEstimate(flops=80 * cells, bytes_accessed=32 * cells, transcendentals=6 * cells),
        name="finish_part",
    )(u, left, right, *others)


def sweep_body(low_ref, mid_ref, high_ref, weight_ref, fixed_ref, low_out, mid_out, high_out):
    tiles, lanes = low_ref.shape[1], low_ref.shape[3]
    layers = mid_ref.shape[0] + 2

    def at(i, t):
        if i == 0:
            return low_ref[0, t]
        if i == layers - 1:
            return high_ref[0, t]
        return mid_ref[i - 1, t]

    def one(i, t, cell, before, after):
        total = before + after + pltpu.roll(cell, lanes - 1, 1) + pltpu.roll(cell, 1, 1)
        if i > 0:
            total = total + at(i - 1, t)
        if i < layers - 1:
            total = total + at(i + 1, t)
        weight = weight_ref[i, t]
        new = weight * fixed_ref[i, t] + (1.0 - weight) * (total * (1.0 / 6.0))
        if i == 0:
            low_out[0, t] = new
        elif i == layers - 1:
            high_out[0, t] = new
        else:
            mid_out[i - 1, t] = new

    for i in range(layers):
        first, final = at(i, 0), at(i, tiles - 1)
        one(i, 0, first, edge_tile(final, first, True), at(i, 1))
        one(i, tiles - 1, final, at(i, tiles - 2), edge_tile(first, final, False))

    def loop(t, carry):
        for i in range(layers):
            one(i, t, at(i, t), at(i, t - 1), at(i, t + 1))
        return carry

    lax.fori_loop(1, tiles - 1, loop, 0)


def sweep_part(low, mid, high, weight, fixed):
    cells = weight.size
    shapes = [jax.ShapeDtypeStruct(v.shape, jnp.float32) for v in (low, mid, high)]
    vmem = pl.BlockSpec(memory_space=pltpu.VMEM)
    return pl.pallas_call(
        sweep_body,
        in_specs=[vmem] * 5,
        out_specs=(vmem, vmem, vmem),
        out_shape=tuple(shapes),
        compiler_params=pltpu.CompilerParams(vmem_limit_bytes=24 * 1024 * 1024),
        cost_estimate=pl.CostEstimate(flops=12 * cells, bytes_accessed=16 * cells, transcendentals=0),
        name="sweep_part",
    )(low, mid, high, weight, fixed)


def fold_rows(array):
    layers, rows, lanes = array.shape
    return array.reshape(layers, SUB, rows // SUB, lanes).transpose(0, 2, 1, 3)


def unfold_rows(array):
    layers, tiles, _, lanes = array.shape
    return array.transpose(0, 2, 1, 3).reshape(layers, tiles * SUB, lanes)


def to_next(array):
    count = lax.axis_size("gx")
    return lax.ppermute(array, "gx", [(i, (i + 1) % count) for i in range(count)])


def to_previous(array):
    count = lax.axis_size("gx")
    return lax.ppermute(array, "gx", [((i + 1) % count, i) for i in range(count)])


def per_device(level_set, sensitivity, band):
    layers = level_set.shape[0]
    weight = fold_rows(band).astype(jnp.float32)
    fixed = weight * fold_rows(sensitivity)
    level = fold_rows(level_set)
    per = level.shape[1] // CHUNKS
    pieces = [level[:, i * per : (i + 1) * per] for i in range(CHUNKS)]
    heads = [piece[:3] for piece in pieces]
    tails = [piece[layers - 3 :] for piece in pieces]

    low, mid, high = fixed[:1], fixed[1 : layers - 1], fixed[layers - 1 :]
    low_open = (1.0 - weight[:1]) * (1.0 / 6.0)
    high_open = (1.0 - weight[layers - 1 :]) * (1.0 / 6.0)
    for sweep in range(SWEEPS):
        from_previous = to_next(high)
        from_next = to_previous(low)
        if sweep == 0:
            halos = [(to_next(tails[i]), to_previous(heads[i])) for i in range(CHUNKS)]
        low_part, mid, high_part = sweep_part(low, mid, high, weight, fixed)
        low = low_part + low_open * from_previous
        high = high_part + high_open * from_next
    speed = jnp.concatenate([low, mid, high], axis=0)

    rise, fall = local_part([level], None)
    kinds = ["first", "second", "third"] + ["reinit"] * REINIT
    base = level
    marker = None
    for number, kind in enumerate(kinds):
        last = number == len(kinds) - 1
        if number > 0:
            halos = [(to_next(tails[i]), to_previous(heads[i])) for i in range(CHUNKS)]
            if kind == "reinit" and marker is None:
                marker = pieces
            if kind == "reinit":
                local = local_part(pieces, jnp.concatenate(marker, axis=1) if CHUNKS > 1 else marker[0])
            else:
                local = local_part(pieces, speed)
        results = []
        for i in range(CHUNKS):
            if kind == "first":
                others = (rise, fall, speed)
            elif kind == "reinit":
                others = (local, marker[i])
            else:
                others = (local, speed, level)
            results.append(finish_part(kind, last, i, pieces[i], halos[i][0], halos[i][1], others))
        if last:
            pieces = results
        else:
            pieces = [r[0] for r in results]
            heads = [r[1] for r in results]
            tails = [r[2] for r in results]
    updated = jnp.concatenate(pieces, axis=1) if CHUNKS > 1 else pieces[0]
    return (unfold_rows(speed), unfold_rows(updated))


def solution(mesh):
    spec = P(("cases", "gx"), None, None)
    return jax.shard_map(
        per_device, mesh=mesh, in_specs=(spec, spec, spec), out_specs=(spec, spec), check_vma=False
    )
```

```python
import functools

import jax
import jax.numpy as jnp
from jax import lax
from jax.experimental import pallas as pl
from jax.experimental.pallas import tpu as pltpu
from jax.sharding import PartitionSpec as P

SWEEPS = 4
REINIT = 2
SUB = 8
CHUNKS = 2

weno_eps = 1e-06
advect_step = 0.15
reinit_step = 0.3


def recip(value):
    return pl.reciprocal(value, approx=True)


def face_pair(d, q6, s4, a, b, c, r_here, r_next):
    ratio_a = b * recip(a)
    ratio_c = b * recip(c)
    gain_a = ratio_a * ratio_a
    gain_c = ratio_c * ratio_c
    part_a = gain_a * r_here
    part_c = gain_c * r_next
    half = 0.5 * (gain_a + gain_c) + 3.0
    mid = d + 0.5 * q6
    minus = (mid + s4) - (part_a + 1.5 * part_c) * recip(half + gain_c)
    negated_plus = (s4 - mid) - (1.5 * part_a + part_c) * recip(half + gain_a)
    return minus, negated_plus


def smoothness(x, y, x_square, y_square):
    cross = x * y
    base = (x_square + y_square) + 0.75 * weno_eps
    outer = base - 2.75 * cross
    return outer + 1.5 * y_square, base - 1.25 * cross, outer + 1.5 * x_square


def along_line(cells):
    count = len(cells) - 6
    d = [cells[i + 1] - cells[i] for i in range(count + 5)]
    e = [d[i + 1] - d[i] for i in range(count + 4)]
    squares = [v * v for v in e]
    triples = [smoothness(e[i], e[i + 1], squares[i], squares[i + 1]) for i in range(count + 3)]
    q6 = [(e[i + 1] - e[i]) * (1.0 / 6.0) for i in range(count + 3)]
    r6 = [q6[i + 1] - q6[i] for i in range(count + 2)]
    faces = []
    for k in range(count + 1):
        s4 = 0.25 * (e[k + 1] + e[k + 2])
        faces.append(
            face_pair(
                d[k + 2], q6[k + 1], s4, triples[k][0], triples[k + 1][1], triples[k + 2][2], r6[k], r6[k + 1]
            )
        )
    return [(faces[i][0], faces[i + 1][1]) for i in range(count)]


def along_lanes(cell):
    length = cell.shape[1]

    def back(v):
        return pltpu.roll(v, 1, 1)

    def ahead(v):
        return pltpu.roll(v, length - 1, 1)

    d = ahead(cell) - cell
    x = d - back(d)
    y = ahead(x)
    a, b, c = smoothness(x, y, x * x, y * y)
    q6 = (y - x) * (1.0 / 6.0)
    r6 = q6 - back(q6)
    minus, negated_plus = face_pair(d, q6, 0.25 * (x + y), back(a), b, ahead(c), r6, ahead(r6))
    return back(minus), negated_plus


def upwind(pair, positive):
    minus, negated_plus = pair
    rising = jnp.maximum(jnp.maximum(minus, negated_plus), 0.0)
    falling = jnp.minimum(jnp.minimum(minus, negated_plus), 0.0)
    chosen = jnp.where(positive, rising, falling)
    return chosen * chosen


def upwind_both(pair):
    minus, negated_plus = pair
    rising = jnp.maximum(jnp.maximum(minus, negated_plus), 0.0)
    falling = jnp.minimum(jnp.minimum(minus, negated_plus), 0.0)
    return rising * rising, falling * falling


def shift_rows(tile, down):
    rows = lax.broadcasted_iota(jnp.int32, tile.shape, 0)
    if down:
        return jnp.where(rows == 0, tile, pltpu.roll(tile, 1, 0))
    return jnp.where(rows == SUB - 1, tile, pltpu.roll(tile, SUB - 1, 0))


def edge_tile(wrapped, nearest_row_tile, low):
    rows = lax.broadcasted_iota(jnp.int32, wrapped.shape, 0)
    if low:
        return jnp.where(rows == 0, nearest_row_tile, pltpu.roll(wrapped, 1, 0))
    return jnp.where(rows == SUB - 1, nearest_row_tile, pltpu.roll(wrapped, SUB - 1, 0))


def local_body(chunks, both, block, *refs):
    u_refs = refs[:chunks]
    if both:
        rise_ref, fall_ref, padded = refs[chunks:]
    else:
        vel_ref, out_ref, padded = refs[chunks:]
    tiles = padded.shape[0] - 6
    per = tiles // chunks
    for index in range(chunks):
        padded[3 + index * per : 3 + (index + 1) * per] = u_refs[index][0]
    first = padded[3]
    final = padded[tiles + 2]
    for step in range(3):
        padded[step] = edge_tile(padded[tiles + step], first, True)
        padded[tiles + 3 + step] = edge_tile(padded[3 + step], final, False)

    def loop(number, carry):
        start = number * block
        cells = [padded[start + i] for i in range(block + 6)]
        pairs = along_line(cells)
        for i in range(block):
            lanes = along_lanes(cells[i + 3])
            if both:
                rise_y, fall_y = upwind_both(pairs[i])
                rise_z, fall_z = upwind_both(lanes)
                rise_ref[0, start + i] = rise_y + rise_z
                fall_ref[0, start + i] = fall_y + fall_z
            else:
                positive = vel_ref[0, start + i] > 0.0
                out_ref[0, start + i] = upwind(pairs[i], positive) + upwind(lanes, positive)
        return carry

    lax.fori_loop(0, tiles // block, loop, 0)


def local_part(pieces, velocity, block=16):
    layers, per, _, lanes = pieces[0].shape
    tiles = per * len(pieces)
    both = velocity is None
    whole = pl.BlockSpec((1, tiles, SUB, lanes), lambda i: (i, 0, 0, 0))
    piece = pl.BlockSpec((1, per, SUB, lanes), lambda i: (i, 0, 0, 0))
    shape = jax.ShapeDtypeStruct((layers, tiles, SUB, lanes), jnp.float32)
    cells = layers * tiles * SUB * lanes
    return pl.pallas_call(
        functools.partial(local_body, len(pieces), both, block),
        grid=(layers,),
        in_specs=[piece] * len(pieces) + ([] if both else [whole]),
        out_specs=(whole, whole) if both else whole,
        out_shape=(shape, shape) if both else shape,
        scratch_shapes=[pltpu.VMEM((tiles + 6, SUB, lanes), jnp.float32)],
        compiler_params=pltpu.CompilerParams(vmem_limit_bytes=24 * 1024 * 1024),
        cost_estimate=pl.CostEstimate(flops=130 * cells, bytes_accessed=12 * cells, transcendentals=8 * cells),
        name="local_part",
    )(*pieces, *(() if both else (velocity,)))


def finish_body(kind, last, *refs):
    u_ref, left_ref, right_ref = refs[:3]
    rest = list(refs[3:])
    layers, tiles = u_ref.shape[0], u_ref.shape[1]
    if kind == "first":
        rise_ref, fall_ref, vel_ref = rest[:3]
        rest = rest[3:]
    else:
        local_ref, vel_ref = rest[:2]
        rest = rest[2:]
        if kind in ("second", "third"):
            base_ref = rest.pop(0)
    out_ref = rest[0]

    def loop(t, carry):
        own = [u_ref[i, t] for i in range(layers)]
        cells = [left_ref[i, t] for i in range(3)] + own + [right_ref[i, t] for i in range(3)]
        pairs = along_line(cells)
        for i in range(layers):
            vel = vel_ref[i, t]
            positive = vel > 0.0
            total = upwind(pairs[i], positive)
            if kind == "first":
                total = total + jnp.where(positive, rise_ref[i, t], fall_ref[i, t])
            else:
                total = total + local_ref[i, t]
            height = jnp.sqrt(total)
            if kind == "first":
                new = own[i] - advect_step * (vel * height)
            elif kind == "second":
                new = 0.75 * base_ref[i, t] + 0.25 * (own[i] - advect_step * (vel * height))
            elif kind == "third":
                new = base_ref[i, t] * (1.0 / 3.0) + (2.0 / 3.0) * (own[i] - advect_step * (vel * height))
            else:
                sign = vel * lax.rsqrt(vel * vel + 1.0)
                new = own[i] - reinit_step * (sign * (height - 1.0))
            out_ref[i, t] = new
            if not last:
                if i < 3:
                    rest[1][i, t] = new
                if i >= layers - 3:
                    rest[2][i - (layers - 3), t] = new
        return carry

    lax.fori_loop(0, tiles, loop, 0)


def finish_part(kind, last, index, u, left, right, others, block=4):
    layers, per, _, lanes = u.shape
    block = min(block, per)
    shift = index * (per // block)
    own = pl.BlockSpec((layers, block, SUB, lanes), lambda i: (0, i, 0, 0))
    side = pl.BlockSpec((3, block, SUB, lanes), lambda i: (0, i, 0, 0))
    moved = pl.BlockSpec((layers, block, SUB, lanes), lambda i: (0, i + shift, 0, 0))
    shape = jax.ShapeDtypeStruct(u.shape, jnp.float32)
    side_shape = jax.ShapeDtypeStruct((3, per, SUB, lanes), jnp.float32)
    specs = [moved if other.shape[1] != per else own for other in others]
    cells = layers * per * SUB * lanes
    return pl.pallas_call(
        functools.partial(finish_body, kind, last),
        grid=(per // block,),
        in_specs=[own, side, side] + specs,
        out_specs=own if last else (own, side, side),
        out_shape=shape if last else (shape, side_shape, side_shape),
        compiler_params=pltpu.CompilerParams(vmem_limit_bytes=24 * 1024 * 1024),
        cost_estimate=pl.CostEstimate(flops=80 * cells, bytes_accessed=32 * cells, transcendentals=6 * cells),
        name="finish_part",
    )(u, left, right, *others)


def sweep_body(low_ref, mid_ref, high_ref, weight_ref, fixed_ref, low_out, mid_out, high_out):
    tiles, lanes = low_ref.shape[1], low_ref.shape[3]
    layers = mid_ref.shape[0] + 2

    def at(i, t):
        if i == 0:
            return low_ref[0, t]
        if i == layers - 1:
            return high_ref[0, t]
        return mid_ref[i - 1, t]

    def one(i, t, cell, before, after):
        total = before + after + pltpu.roll(cell, lanes - 1, 1) + pltpu.roll(cell, 1, 1)
        if i > 0:
            total = total + at(i - 1, t)
        if i < layers - 1:
            total = total + at(i + 1, t)
        weight = weight_ref[i, t]
        new = weight * fixed_ref[i, t] + (1.0 - weight) * (total * (1.0 / 6.0))
        if i == 0:
            low_out[0, t] = new
        elif i == layers - 1:
            high_out[0, t] = new
        else:
            mid_out[i - 1, t] = new

    for i in range(layers):
        first, final = at(i, 0), at(i, tiles - 1)
        one(i, 0, first, edge_tile(final, first, True), at(i, 1))
        one(i, tiles - 1, final, at(i, tiles - 2), edge_tile(first, final, False))

    def loop(t, carry):
        for i in range(layers):
            one(i, t, at(i, t), at(i, t - 1), at(i, t + 1))
        return carry

    lax.fori_loop(1, tiles - 1, loop, 0, unroll=5)


def sweep_part(low, mid, high, weight, fixed):
    cells = weight.size
    shapes = [jax.ShapeDtypeStruct(v.shape, jnp.float32) for v in (low, mid, high)]
    vmem = pl.BlockSpec(memory_space=pltpu.VMEM)
    return pl.pallas_call(
        sweep_body,
        in_specs=[vmem] * 5,
        out_specs=(vmem, vmem, vmem),
        out_shape=tuple(shapes),
        compiler_params=pltpu.CompilerParams(vmem_limit_bytes=24 * 1024 * 1024),
        cost_estimate=pl.CostEstimate(flops=12 * cells, bytes_accessed=16 * cells, transcendentals=0),
        name="sweep_part",
    )(low, mid, high, weight, fixed)


def fold_rows(array):
    layers, rows, lanes = array.shape
    return array.reshape(layers, SUB, rows // SUB, lanes).transpose(0, 2, 1, 3)


def unfold_rows(array):
    layers, tiles, _, lanes = array.shape
    return array.transpose(0, 2, 1, 3).reshape(layers, tiles * SUB, lanes)


def to_next(array):
    count = lax.axis_size("gx")
    return lax.ppermute(array, "gx", [(i, (i + 1) % count) for i in range(count)])


def to_previous(array):
    count = lax.axis_size("gx")
    return lax.ppermute(array, "gx", [((i + 1) % count, i) for i in range(count)])


def per_device(level_set, sensitivity, band):
    layers = level_set.shape[0]
    weight = fold_rows(band).astype(jnp.float32)
    fixed = weight * fold_rows(sensitivity)
    level = fold_rows(level_set)
    per = level.shape[1] // CHUNKS
    pieces = [level[:, i * per : (i + 1) * per] for i in range(CHUNKS)]
    heads = [piece[:3] for piece in pieces]
    tails = [piece[layers - 3 :] for piece in pieces]

    low, mid, high = fixed[:1], fixed[1 : layers - 1], fixed[layers - 1 :]
    low_open = (1.0 - weight[:1]) * (1.0 / 6.0)
    high_open = (1.0 - weight[layers - 1 :]) * (1.0 / 6.0)
    for sweep in range(SWEEPS):
        from_previous = to_next(high)
        from_next = to_previous(low)
        if sweep == 0:
            halos = [(to_next(tails[i]), to_previous(heads[i])) for i in range(CHUNKS)]
        low_part, mid, high_part = sweep_part(low, mid, high, weight, fixed)
        low = low_part + low_open * from_previous
        high = high_part + high_open * from_next
    speed = jnp.concatenate([low, mid, high], axis=0)

    rise, fall = local_part([level], None)
    kinds = ["first", "second", "third"] + ["reinit"] * REINIT
    base = level
    marker = None
    for number, kind in enumerate(kinds):
        last = number == len(kinds) - 1
        if number > 0:
            halos = [(to_next(tails[i]), to_previous(heads[i])) for i in range(CHUNKS)]
            if kind == "reinit" and marker is None:
                marker = pieces
            if kind == "reinit":
                local = local_part(pieces, jnp.concatenate(marker, axis=1) if CHUNKS > 1 else marker[0])
            else:
                local = local_part(pieces, speed)
        results = []
        for i in range(CHUNKS):
            if kind == "first":
                others = (rise, fall, speed)
            elif kind == "reinit":
                others = (local, marker[i])
            else:
                others = (local, speed, level)
            results.append(finish_part(kind, last, i, pieces[i], halos[i][0], halos[i][1], others))
        if last:
            pieces = results
        else:
            pieces = [r[0] for r in results]
            heads = [r[1] for r in results]
            tails = [r[2] for r in results]
    updated = jnp.concatenate(pieces, axis=1) if CHUNKS > 1 else pieces[0]
    return (unfold_rows(speed), unfold_rows(updated))


def solution(mesh):
    spec = P(("cases", "gx"), None, None)
    return jax.shard_map(
        per_device, mesh=mesh, in_specs=(spec, spec, spec), out_specs=(spec, spec), check_vma=False
    )
```

```python
import functools

import jax
import jax.numpy as jnp
from jax import lax
from jax.experimental import pallas as pl
from jax.experimental.pallas import tpu as pltpu
from jax.sharding import PartitionSpec as P

SWEEPS = 4
REINIT = 2
SUB = 8
SPLIT = (0, 4, 8)

weno_eps = 1e-06
advect_step = 0.15
reinit_step = 0.3


def recip(value):
    return pl.reciprocal(value, approx=True)


def face_pair(d, q6, s4, a, b, c, r_here, r_next):
    ratio_a = b * recip(a)
    ratio_c = b * recip(c)
    gain_a = ratio_a * ratio_a
    gain_c = ratio_c * ratio_c
    part_a = gain_a * r_here
    part_c = gain_c * r_next
    half = 0.5 * (gain_a + gain_c) + 3.0
    mid = d + 0.5 * q6
    minus = (mid + s4) - (part_a + 1.5 * part_c) * recip(half + gain_c)
    negated_plus = (s4 - mid) - (1.5 * part_a + part_c) * recip(half + gain_a)
    return minus, negated_plus


def smoothness(x, y, x_square, y_square):
    cross = x * y
    base = (x_square + y_square) + 0.75 * weno_eps
    outer = base - 2.75 * cross
    return outer + 1.5 * y_square, base - 1.25 * cross, outer + 1.5 * x_square


def along_line(cells):
    count = len(cells) - 6
    d = [cells[i + 1] - cells[i] for i in range(count + 5)]
    e = [d[i + 1] - d[i] for i in range(count + 4)]
    squares = [v * v for v in e]
    triples = [smoothness(e[i], e[i + 1], squares[i], squares[i + 1]) for i in range(count + 3)]
    q6 = [(e[i + 1] - e[i]) * (1.0 / 6.0) for i in range(count + 3)]
    r6 = [q6[i + 1] - q6[i] for i in range(count + 2)]
    faces = []
    for k in range(count + 1):
        s4 = 0.25 * (e[k + 1] + e[k + 2])
        faces.append(
            face_pair(
                d[k + 2], q6[k + 1], s4, triples[k][0], triples[k + 1][1], triples[k + 2][2], r6[k], r6[k + 1]
            )
        )
    return [(faces[i][0], faces[i + 1][1]) for i in range(count)]


def along_lanes(cell):
    length = cell.shape[1]

    def back(v):
        return pltpu.roll(v, 1, 1)

    def ahead(v):
        return pltpu.roll(v, length - 1, 1)

    d = ahead(cell) - cell
    x = d - back(d)
    y = ahead(x)
    a, b, c = smoothness(x, y, x * x, y * y)
    q6 = (y - x) * (1.0 / 6.0)
    r6 = q6 - back(q6)
    minus, negated_plus = face_pair(d, q6, 0.25 * (x + y), back(a), b, ahead(c), r6, ahead(r6))
    return back(minus), negated_plus


def upwind(pair, positive):
    minus, negated_plus = pair
    rising = jnp.maximum(jnp.maximum(minus, negated_plus), 0.0)
    falling = jnp.minimum(jnp.minimum(minus, negated_plus), 0.0)
    chosen = jnp.where(positive, rising, falling)
    return chosen * chosen


def upwind_both(pair):
    minus, negated_plus = pair
    rising = jnp.maximum(jnp.maximum(minus, negated_plus), 0.0)
    falling = jnp.minimum(jnp.minimum(minus, negated_plus), 0.0)
    return rising * rising, falling * falling


def shift_rows(tile, down):
    rows = lax.broadcasted_iota(jnp.int32, tile.shape, 0)
    if down:
        return jnp.where(rows == 0, tile, pltpu.roll(tile, 1, 0))
    return jnp.where(rows == SUB - 1, tile, pltpu.roll(tile, SUB - 1, 0))


def edge_tile(wrapped, nearest_row_tile, low):
    rows = lax.broadcasted_iota(jnp.int32, wrapped.shape, 0)
    if low:
        return jnp.where(rows == 0, nearest_row_tile, pltpu.roll(wrapped, 1, 0))
    return jnp.where(rows == SUB - 1, nearest_row_tile, pltpu.roll(wrapped, SUB - 1, 0))


def local_body(chunks, both, block, *refs):
    u_refs = refs[:chunks]
    if both:
        rise_ref, fall_ref, padded = refs[chunks:]
    else:
        vel_ref, out_ref, padded = refs[chunks:]
    tiles = padded.shape[0] - 6
    start = 3
    for ref in u_refs:
        padded[start : start + ref.shape[1]] = ref[0]
        start += ref.shape[1]
    first = padded[3]
    final = padded[tiles + 2]
    for step in range(3):
        padded[step] = edge_tile(padded[tiles + step], first, True)
        padded[tiles + 3 + step] = edge_tile(padded[3 + step], final, False)

    def loop(number, carry):
        start = number * block
        cells = [padded[start + i] for i in range(block + 6)]
        pairs = along_line(cells)
        for i in range(block):
            lanes = along_lanes(cells[i + 3])
            if both:
                rise_y, fall_y = upwind_both(pairs[i])
                rise_z, fall_z = upwind_both(lanes)
                rise_ref[0, start + i] = rise_y + rise_z
                fall_ref[0, start + i] = fall_y + fall_z
            else:
                positive = vel_ref[0, start + i] > 0.0
                out_ref[0, start + i] = upwind(pairs[i], positive) + upwind(lanes, positive)
        return carry

    lax.fori_loop(0, tiles // block, loop, 0)


def local_part(pieces, velocity, block=16):
    layers, _, _, lanes = pieces[0].shape
    tiles = sum(piece.shape[1] for piece in pieces)
    both = velocity is None
    whole = pl.BlockSpec((1, tiles, SUB, lanes), lambda i: (i, 0, 0, 0))
    shape = jax.ShapeDtypeStruct((layers, tiles, SUB, lanes), jnp.float32)
    cells = layers * tiles * SUB * lanes
    return pl.pallas_call(
        functools.partial(local_body, len(pieces), both, block),
        grid=(layers,),
        in_specs=[pl.BlockSpec((1,) + p.shape[1:], lambda i: (i, 0, 0, 0)) for p in pieces] + ([] if both else [whole]),
        out_specs=(whole, whole) if both else whole,
        out_shape=(shape, shape) if both else shape,
        scratch_shapes=[pltpu.VMEM((tiles + 6, SUB, lanes), jnp.float32)],
        compiler_params=pltpu.CompilerParams(vmem_limit_bytes=24 * 1024 * 1024),
        cost_estimate=pl.CostEstimate(flops=130 * cells, bytes_accessed=12 * cells, transcendentals=8 * cells),
        name="local_part",
    )(*pieces, *(() if both else (velocity,)))


def finish_body(kind, last, *refs):
    parity_ref, u_ref, far_ref, near_ref = refs[:4]
    rest = list(refs[4:])
    even = parity_ref[0] == 0
    layers, tiles = u_ref.shape[0], u_ref.shape[1]
    if kind == "first":
        rise_ref, fall_ref, vel_ref = rest[:3]
        rest = rest[3:]
    else:
        local_ref, vel_ref = rest[:2]
        rest = rest[2:]
        if kind in ("second", "third"):
            base_ref = rest.pop(0)
    out_ref = rest[0]

    def loop(t, carry):
        own = [u_ref[i, t] for i in range(layers)]
        far = [far_ref[i, t] for i in range(3)]
        near = [near_ref[i, t] for i in range(3)]
        cells = [jnp.where(even, a, b) for a, b in zip(far, near)] + own + [jnp.where(even, b, a) for a, b in zip(far, near)]
        made = []
        pairs = along_line(cells)
        for i in range(layers):
            vel = vel_ref[i, t]
            positive = vel > 0.0
            total = upwind(pairs[i], positive)
            if kind == "first":
                total = total + jnp.where(positive, rise_ref[i, t], fall_ref[i, t])
            else:
                total = total + local_ref[i, t]
            height = jnp.sqrt(total)
            if kind == "first":
                new = own[i] - advect_step * (vel * height)
            elif kind == "second":
                new = 0.75 * base_ref[i, t] + 0.25 * (own[i] - advect_step * (vel * height))
            elif kind == "third":
                new = base_ref[i, t] * (1.0 / 3.0) + (2.0 / 3.0) * (own[i] - advect_step * (vel * height))
            else:
                sign = vel * lax.rsqrt(vel * vel + 1.0)
                new = own[i] - reinit_step * (sign * (height - 1.0))
            out_ref[i, t] = new
            made.append(new)
        if not last:
            for i in range(3):
                rest[1][i, t] = jnp.where(even, made[i], made[layers - 3 + i])
                rest[2][i, t] = jnp.where(even, made[layers - 3 + i], made[i])
        return carry

    lax.fori_loop(0, tiles, loop, 0)


def finish_part(kind, last, start, parity, u, far, near, others, block=4):
    layers, per, _, lanes = u.shape
    block = min(block, per)
    shift = start // block
    own = pl.BlockSpec((layers, block, SUB, lanes), lambda i: (0, i, 0, 0))
    side = pl.BlockSpec((3, block, SUB, lanes), lambda i: (0, i, 0, 0))
    moved = pl.BlockSpec((layers, block, SUB, lanes), lambda i: (0, i + shift, 0, 0))
    shape = jax.ShapeDtypeStruct(u.shape, jnp.float32)
    side_shape = jax.ShapeDtypeStruct((3, per, SUB, lanes), jnp.float32)
    specs = [moved if other.shape[1] != per else own for other in others]
    cells = layers * per * SUB * lanes
    return pl.pallas_call(
        functools.partial(finish_body, kind, last),
        grid=(per // block,),
        in_specs=[pl.BlockSpec(memory_space=pltpu.SMEM), own, side, side] + specs,
        out_specs=own if last else (own, side, side),
        out_shape=shape if last else (shape, side_shape, side_shape),
        compiler_params=pltpu.CompilerParams(vmem_limit_bytes=24 * 1024 * 1024),
        cost_estimate=pl.CostEstimate(flops=80 * cells, bytes_accessed=32 * cells, transcendentals=6 * cells),
        name="finish_part",
    )(parity, u, far, near, *others)


def sweep_body(parity_ref, far_ref, mid_ref, near_ref, weight_ref, fixed_ref, far_out, mid_out, near_out, padded):
    layers, tiles, lanes = weight_ref.shape[0], weight_ref.shape[1], weight_ref.shape[3]
    even = parity_ref[0] == 0
    padded[jnp.where(even, 0, layers - 1), 1 : tiles + 1] = far_ref[0]
    padded[jnp.where(even, layers - 1, 0), 1 : tiles + 1] = near_ref[0]
    for i in range(1, layers - 1):
        padded[i, 1 : tiles + 1] = mid_ref[i - 1]
    for i in range(layers):
        first, final = padded[i, 1], padded[i, tiles]
        padded[i, 0] = edge_tile(final, first, True)
        padded[i, tiles + 1] = edge_tile(first, final, False)

    def loop(t, carry):
        cells = [padded[i, t + 1] for i in range(layers)]
        ends = []
        for i in range(layers):
            total = padded[i, t] + padded[i, t + 2]
            total = total + pltpu.roll(cells[i], lanes - 1, 1) + pltpu.roll(cells[i], 1, 1)
            if i > 0:
                total = total + cells[i - 1]
            if i < layers - 1:
                total = total + cells[i + 1]
            weight = weight_ref[i, t]
            new = weight * fixed_ref[i, t] + (1.0 - weight) * (total * (1.0 / 6.0))
            if 0 < i < layers - 1:
                mid_out[i - 1, t] = new
            else:
                ends.append(new)
        far_out[0, t] = jnp.where(even, ends[0], ends[1])
        near_out[0, t] = jnp.where(even, ends[1], ends[0])
        return carry

    lax.fori_loop(0, tiles, loop, 0, unroll=4)


def sweep_part(parity, far, mid, near, weight, fixed):
    cells = weight.size
    layers, tiles, _, lanes = weight.shape
    vmem = pl.BlockSpec(memory_space=pltpu.VMEM)
    return pl.pallas_call(
        sweep_body,
        in_specs=[pl.BlockSpec(memory_space=pltpu.SMEM)] + [vmem] * 5,
        out_specs=(vmem, vmem, vmem),
        out_shape=tuple(jax.ShapeDtypeStruct(v.shape, jnp.float32) for v in (far, mid, near)),
        scratch_shapes=[pltpu.VMEM((layers, tiles + 2, SUB, lanes), jnp.float32)],
        compiler_params=pltpu.CompilerParams(vmem_limit_bytes=24 * 1024 * 1024),
        cost_estimate=pl.CostEstimate(flops=12 * cells, bytes_accessed=16 * cells, transcendentals=0),
        name="sweep_part",
    )(parity, far, mid, near, weight, fixed)


def fold_rows(array):
    layers, rows, lanes = array.shape
    return array.reshape(layers, SUB, rows // SUB, lanes).transpose(0, 2, 1, 3)


def unfold_rows(array):
    layers, tiles, _, lanes = array.shape
    return array.transpose(0, 2, 1, 3).reshape(layers, tiles * SUB, lanes)


def swap_far(array):
    count = lax.axis_size("gx")
    odd = range(1, count, 2)
    return lax.ppermute(array, "gx", [(i, (i + 1) % count) for i in odd] + [((i + 1) % count, i) for i in odd])


def swap_near(array):
    count = lax.axis_size("gx")
    return lax.ppermute(array, "gx", [(i, i + 1 - 2 * (i % 2)) for i in range(count)])


def per_device(level_set, sensitivity, band):
    layers = level_set.shape[0]
    weight = fold_rows(band).astype(jnp.float32)
    fixed = weight * fold_rows(sensitivity)
    level = fold_rows(level_set)
    bounds = [level.shape[1] * part // 8 for part in SPLIT]

    def cut(array):
        return [array[:, start:stop] for start, stop in zip(bounds, bounds[1:])]

    pieces = cut(level)
    parity = lax.rem(lax.axis_index("gx"), 2)
    even = parity == 0
    parity = parity.astype(jnp.int32).reshape(1)

    def order(first, second):
        return jnp.where(even, first, second), jnp.where(even, second, first)

    sides = list(zip(*[cut(side) for side in order(level[:3], level[layers - 3 :])]))

    edges = [slice(0, 1), slice(layers - 1, layers)]
    far, near = order(*[fold_rows(band[e].astype(jnp.float32) * sensitivity[e]) for e in edges])
    far_open, near_open = order(*[(1.0 - fold_rows(band[e]).astype(jnp.float32)) * (1.0 / 6.0) for e in edges])
    mid = fixed[1 : layers - 1]
    halos = [(swap_far(side[0]), swap_near(side[1])) for side in sides]
    rise, fall = local_part([level], None)
    for sweep in range(SWEEPS):
        from_far, from_near = swap_far(far), swap_near(near)
        far_part, mid, near_part = sweep_part(parity, far, mid, near, weight, fixed)
        if sweep == 1:
            mid, rise, fall = lax.optimization_barrier((mid, rise, fall))
        far = far_part + far_open * from_far
        near = near_part + near_open * from_near
    low, high = order(far, near)
    speed = jnp.concatenate([low, mid, high], axis=0)

    kinds = ["first", "second", "third"] + ["reinit"] * REINIT
    base = level
    marker = None
    for number, kind in enumerate(kinds):
        last = number == len(kinds) - 1
        if number > 0:
            halos = [(swap_far(far), swap_near(near)) for far, near in sides]
            if kind == "reinit" and marker is None:
                marker = pieces
            if kind == "reinit":
                local = local_part(pieces, jnp.concatenate(marker, axis=1))
            else:
                local = local_part(pieces, speed)
        results = []
        for i in range(len(pieces)):
            if kind == "first":
                others = (rise, fall, speed)
            elif kind == "reinit":
                others = (local, marker[i])
            else:
                others = (local, speed, level)
            results.append(finish_part(kind, last, bounds[i], parity, pieces[i], halos[i][0], halos[i][1], others))
        if last:
            pieces = results
        else:
            pieces = [r[0] for r in results]
            sides = [r[1:] for r in results]
    updated = jnp.concatenate(pieces, axis=1)
    return (unfold_rows(speed), unfold_rows(updated))


def solution(mesh):
    spec = P(("cases", "gx"), None, None)
    return jax.shard_map(
        per_device, mesh=mesh, in_specs=(spec, spec, spec), out_specs=(spec, spec), check_vma=False
    )
```

```python
import functools

import jax
import jax.numpy as jnp
from jax import lax
from jax.experimental import pallas as pl
from jax.experimental.pallas import tpu as pltpu
from jax.sharding import PartitionSpec as P

SWEEPS = 4
REINIT = 2
SUB = 8
SPLIT = (0, 4, 8)

weno_eps = 1e-06
advect_step = 0.15
reinit_step = 0.3


def recip(value):
    return pl.reciprocal(value, approx=True)


def face_pair(d, q6, s4, a, b, c, r_here, r_next):
    ratio_a = b * recip(a)
    ratio_c = b * recip(c)
    gain_a = ratio_a * ratio_a
    gain_c = ratio_c * ratio_c
    part_a = gain_a * r_here
    part_c = gain_c * r_next
    half = 0.5 * (gain_a + gain_c) + 3.0
    mid = d + 0.5 * q6
    minus = (mid + s4) - (part_a + 1.5 * part_c) * recip(half + gain_c)
    negated_plus = (s4 - mid) - (1.5 * part_a + part_c) * recip(half + gain_a)
    return minus, negated_plus


def smoothness(x, y, x_square, y_square):
    cross = x * y
    base = (x_square + y_square) + 0.75 * weno_eps
    outer = base - 2.75 * cross
    return outer + 1.5 * y_square, base - 1.25 * cross, outer + 1.5 * x_square


def along_line(cells):
    count = len(cells) - 6
    d = [cells[i + 1] - cells[i] for i in range(count + 5)]
    e = [d[i + 1] - d[i] for i in range(count + 4)]
    squares = [v * v for v in e]
    triples = [smoothness(e[i], e[i + 1], squares[i], squares[i + 1]) for i in range(count + 3)]
    q6 = [(e[i + 1] - e[i]) * (1.0 / 6.0) for i in range(count + 3)]
    r6 = [q6[i + 1] - q6[i] for i in range(count + 2)]
    faces = []
    for k in range(count + 1):
        s4 = 0.25 * (e[k + 1] + e[k + 2])
        faces.append(
            face_pair(
                d[k + 2], q6[k + 1], s4, triples[k][0], triples[k + 1][1], triples[k + 2][2], r6[k], r6[k + 1]
            )
        )
    return [(faces[i][0], faces[i + 1][1]) for i in range(count)]


def along_lanes(cell):
    length = cell.shape[1]

    def back(v):
        return pltpu.roll(v, 1, 1)

    def ahead(v):
        return pltpu.roll(v, length - 1, 1)

    d = ahead(cell) - cell
    x = d - back(d)
    y = ahead(x)
    a, b, c = smoothness(x, y, x * x, y * y)
    q6 = (y - x) * (1.0 / 6.0)
    r6 = q6 - back(q6)
    minus, negated_plus = face_pair(d, q6, 0.25 * (x + y), back(a), b, ahead(c), r6, ahead(r6))
    return back(minus), negated_plus


def upwind(pair, positive):
    minus, negated_plus = pair
    rising = jnp.maximum(jnp.maximum(minus, negated_plus), 0.0)
    falling = jnp.minimum(jnp.minimum(minus, negated_plus), 0.0)
    chosen = jnp.where(positive, rising, falling)
    return chosen * chosen


def upwind_both(pair):
    minus, negated_plus = pair
    rising = jnp.maximum(jnp.maximum(minus, negated_plus), 0.0)
    falling = jnp.minimum(jnp.minimum(minus, negated_plus), 0.0)
    return rising * rising, falling * falling


def shift_rows(tile, down):
    rows = lax.broadcasted_iota(jnp.int32, tile.shape, 0)
    if down:
        return jnp.where(rows == 0, tile, pltpu.roll(tile, 1, 0))
    return jnp.where(rows == SUB - 1, tile, pltpu.roll(tile, SUB - 1, 0))


def edge_tile(wrapped, nearest_row_tile, low):
    rows = lax.broadcasted_iota(jnp.int32, wrapped.shape, 0)
    if low:
        return jnp.where(rows == 0, nearest_row_tile, pltpu.roll(wrapped, 1, 0))
    return jnp.where(rows == SUB - 1, nearest_row_tile, pltpu.roll(wrapped, SUB - 1, 0))


def local_body(chunks, both, block, *refs):
    u_refs = refs[:chunks]
    if both:
        rise_ref, fall_ref, padded = refs[chunks:]
    else:
        vel_ref, out_ref, padded = refs[chunks:]
    tiles = padded.shape[0] - 6
    start = 3
    for ref in u_refs:
        padded[start : start + ref.shape[1]] = ref[0]
        start += ref.shape[1]
    first = padded[3]
    final = padded[tiles + 2]
    for step in range(3):
        padded[step] = edge_tile(padded[tiles + step], first, True)
        padded[tiles + 3 + step] = edge_tile(padded[3 + step], final, False)

    def loop(number, carry):
        start = number * block
        cells = [padded[start + i] for i in range(block + 6)]
        pairs = along_line(cells)
        for i in range(block):
            lanes = along_lanes(cells[i + 3])
            if both:
                rise_y, fall_y = upwind_both(pairs[i])
                rise_z, fall_z = upwind_both(lanes)
                rise_ref[0, start + i] = rise_y + rise_z
                fall_ref[0, start + i] = fall_y + fall_z
            else:
                positive = vel_ref[0, start + i] > 0.0
                out_ref[0, start + i] = upwind(pairs[i], positive) + upwind(lanes, positive)
        return carry

    lax.fori_loop(0, tiles // block, loop, 0)


def local_part(pieces, velocity, block=16):
    layers, _, _, lanes = pieces[0].shape
    tiles = sum(piece.shape[1] for piece in pieces)
    both = velocity is None
    whole = pl.BlockSpec((1, tiles, SUB, lanes), lambda i: (i, 0, 0, 0))
    shape = jax.ShapeDtypeStruct((layers, tiles, SUB, lanes), jnp.float32)
    cells = layers * tiles * SUB * lanes
    return pl.pallas_call(
        functools.partial(local_body, len(pieces), both, block),
        grid=(layers,),
        in_specs=[pl.BlockSpec((1,) + p.shape[1:], lambda i: (i, 0, 0, 0)) for p in pieces] + ([] if both else [whole]),
        out_specs=(whole, whole) if both else whole,
        out_shape=(shape, shape) if both else shape,
        scratch_shapes=[pltpu.VMEM((tiles + 6, SUB, lanes), jnp.float32)],
        compiler_params=pltpu.CompilerParams(vmem_limit_bytes=24 * 1024 * 1024),
        cost_estimate=pl.CostEstimate(flops=130 * cells, bytes_accessed=12 * cells, transcendentals=8 * cells),
        name="local_part",
    )(*pieces, *(() if both else (velocity,)))


def finish_body(kind, last, *refs):
    parity_ref, u_ref, far_ref, near_ref = refs[:4]
    rest = list(refs[4:])
    even = parity_ref[0] == 0
    layers, tiles = u_ref.shape[0], u_ref.shape[1]
    if kind == "first":
        rise_ref, fall_ref, vel_ref = rest[:3]
        rest = rest[3:]
    else:
        local_ref, vel_ref = rest[:2]
        rest = rest[2:]
        if kind in ("second", "third"):
            base_ref = rest.pop(0)
    out_ref = rest[0]

    def loop(t, carry):
        own = [u_ref[i, t] for i in range(layers)]
        far = [far_ref[i, t] for i in range(3)]
        near = [near_ref[i, t] for i in range(3)]
        cells = [jnp.where(even, a, b) for a, b in zip(far, near)] + own + [jnp.where(even, b, a) for a, b in zip(far, near)]
        made = []
        pairs = along_line(cells)
        for i in range(layers):
            vel = vel_ref[i, t]
            positive = vel > 0.0
            total = upwind(pairs[i], positive)
            if kind == "first":
                total = total + jnp.where(positive, rise_ref[i, t], fall_ref[i, t])
            else:
                total = total + local_ref[i, t]
            height = jnp.sqrt(total)
            if kind == "first":
                new = own[i] - advect_step * (vel * height)
            elif kind == "second":
                new = 0.75 * base_ref[i, t] + 0.25 * (own[i] - advect_step * (vel * height))
            elif kind == "third":
                new = base_ref[i, t] * (1.0 / 3.0) + (2.0 / 3.0) * (own[i] - advect_step * (vel * height))
            else:
                sign = vel * lax.rsqrt(vel * vel + 1.0)
                new = own[i] - reinit_step * (sign * (height - 1.0))
            out_ref[i, t] = new
            made.append(new)
        if not last:
            for i in range(3):
                rest[1][i, t] = jnp.where(even, made[i], made[layers - 3 + i])
                rest[2][i, t] = jnp.where(even, made[layers - 3 + i], made[i])
        return carry

    lax.fori_loop(0, tiles, loop, 0, unroll=4)


def finish_part(kind, last, start, parity, u, far, near, others, block=4):
    layers, per, _, lanes = u.shape
    block = min(block, per)
    shift = start // block
    own = pl.BlockSpec((layers, block, SUB, lanes), lambda i: (0, i, 0, 0))
    side = pl.BlockSpec((3, block, SUB, lanes), lambda i: (0, i, 0, 0))
    moved = pl.BlockSpec((layers, block, SUB, lanes), lambda i: (0, i + shift, 0, 0))
    shape = jax.ShapeDtypeStruct(u.shape, jnp.float32)
    side_shape = jax.ShapeDtypeStruct((3, per, SUB, lanes), jnp.float32)
    specs = [moved if other.shape[1] != per else own for other in others]
    cells = layers * per * SUB * lanes
    return pl.pallas_call(
        functools.partial(finish_body, kind, last),
        grid=(per // block,),
        in_specs=[pl.BlockSpec(memory_space=pltpu.SMEM), own, side, side] + specs,
        out_specs=own if last else (own, side, side),
        out_shape=shape if last else (shape, side_shape, side_shape),
        compiler_params=pltpu.CompilerParams(vmem_limit_bytes=24 * 1024 * 1024),
        cost_estimate=pl.CostEstimate(flops=80 * cells, bytes_accessed=32 * cells, transcendentals=6 * cells),
        name="finish_part",
    )(parity, u, far, near, *others)


def sweep_body(parity_ref, far_ref, mid_ref, near_ref, weight_ref, fixed_ref, far_out, mid_out, near_out, padded):
    layers, tiles, lanes = weight_ref.shape[0], weight_ref.shape[1], weight_ref.shape[3]
    even = parity_ref[0] == 0
    padded[jnp.where(even, 0, layers - 1), 1 : tiles + 1] = far_ref[0]
    padded[jnp.where(even, layers - 1, 0), 1 : tiles + 1] = near_ref[0]
    for i in range(1, layers - 1):
        padded[i, 1 : tiles + 1] = mid_ref[i - 1]
    for i in range(layers):
        first, final = padded[i, 1], padded[i, tiles]
        padded[i, 0] = edge_tile(final, first, True)
        padded[i, tiles + 1] = edge_tile(first, final, False)

    def loop(t, carry):
        cells = [padded[i, t + 1] for i in range(layers)]
        ends = []
        for i in range(layers):
            total = padded[i, t] + padded[i, t + 2]
            total = total + pltpu.roll(cells[i], lanes - 1, 1) + pltpu.roll(cells[i], 1, 1)
            if i > 0:
                total = total + cells[i - 1]
            if i < layers - 1:
                total = total + cells[i + 1]
            weight = weight_ref[i, t]
            new = weight * fixed_ref[i, t] + (1.0 - weight) * (total * (1.0 / 6.0))
            if 0 < i < layers - 1:
                mid_out[i - 1, t] = new
            else:
                ends.append(new)
        far_out[0, t] = jnp.where(even, ends[0], ends[1])
        near_out[0, t] = jnp.where(even, ends[1], ends[0])
        return carry

    lax.fori_loop(0, tiles, loop, 0, unroll=4)


def sweep_part(parity, far, mid, near, weight, fixed):
    cells = weight.size
    layers, tiles, _, lanes = weight.shape
    vmem = pl.BlockSpec(memory_space=pltpu.VMEM)
    return pl.pallas_call(
        sweep_body,
        in_specs=[pl.BlockSpec(memory_space=pltpu.SMEM)] + [vmem] * 5,
        out_specs=(vmem, vmem, vmem),
        out_shape=tuple(jax.ShapeDtypeStruct(v.shape, jnp.float32) for v in (far, mid, near)),
        scratch_shapes=[pltpu.VMEM((layers, tiles + 2, SUB, lanes), jnp.float32)],
        compiler_params=pltpu.CompilerParams(vmem_limit_bytes=24 * 1024 * 1024),
        cost_estimate=pl.CostEstimate(flops=12 * cells, bytes_accessed=16 * cells, transcendentals=0),
        name="sweep_part",
    )(parity, far, mid, near, weight, fixed)


def fold_rows(array):
    layers, rows, lanes = array.shape
    return array.reshape(layers, SUB, rows // SUB, lanes).transpose(0, 2, 1, 3)


def unfold_rows(array):
    layers, tiles, _, lanes = array.shape
    return array.transpose(0, 2, 1, 3).reshape(layers, tiles * SUB, lanes)


def swap_far(array):
    count = lax.axis_size("gx")
    odd = range(1, count, 2)
    return lax.ppermute(array, "gx", [(i, (i + 1) % count) for i in odd] + [((i + 1) % count, i) for i in odd])


def swap_near(array):
    count = lax.axis_size("gx")
    return lax.ppermute(array, "gx", [(i, i + 1 - 2 * (i % 2)) for i in range(count)])


def per_device(level_set, sensitivity, band):
    layers = level_set.shape[0]
    weight = fold_rows(band).astype(jnp.float32)
    fixed = weight * fold_rows(sensitivity)
    level = fold_rows(level_set)
    bounds = [level.shape[1] * part // 8 for part in SPLIT]

    def cut(array):
        return [array[:, start:stop] for start, stop in zip(bounds, bounds[1:])]

    pieces = cut(level)
    parity = lax.rem(lax.axis_index("gx"), 2)
    even = parity == 0
    parity = parity.astype(jnp.int32).reshape(1)

    def order(first, second):
        return jnp.where(even, first, second), jnp.where(even, second, first)

    sides = list(zip(*[cut(side) for side in order(level[:3], level[layers - 3 :])]))

    edges = [slice(0, 1), slice(layers - 1, layers)]
    far, near = order(*[fold_rows(band[e].astype(jnp.float32) * sensitivity[e]) for e in edges])
    far_open, near_open = order(*[(1.0 - fold_rows(band[e]).astype(jnp.float32)) * (1.0 / 6.0) for e in edges])
    mid = fixed[1 : layers - 1]
    halos = [(swap_far(side[0]), swap_near(side[1])) for side in sides]
    rise, fall = local_part([level], None)
    for sweep in range(SWEEPS):
        from_far, from_near = swap_far(far), swap_near(near)
        far_part, mid, near_part = sweep_part(parity, far, mid, near, weight, fixed)
        if sweep == 0:
            mid, rise, fall = lax.optimization_barrier((mid, rise, fall))
        far = far_part + far_open * from_far
        near = near_part + near_open * from_near
    low, high = order(far, near)
    speed = jnp.concatenate([low, mid, high], axis=0)

    kinds = ["first", "second", "third"] + ["reinit"] * REINIT
    base = level
    marker = None
    for number, kind in enumerate(kinds):
        last = number == len(kinds) - 1
        if number > 0:
            halos = [(swap_far(far), swap_near(near)) for far, near in sides]
            if kind == "reinit" and marker is None:
                marker = pieces
            if kind == "reinit":
                local = local_part(pieces, jnp.concatenate(marker, axis=1))
            else:
                local = local_part(pieces, speed)
        results = []
        for i in range(len(pieces)):
            if kind == "first":
                others = (rise, fall, speed)
            elif kind == "reinit":
                others = (local, marker[i])
            else:
                others = (local, speed, level)
            results.append(finish_part(kind, last, bounds[i], parity, pieces[i], halos[i][0], halos[i][1], others))
        if last:
            pieces = results
        else:
            pieces = [r[0] for r in results]
            sides = [r[1:] for r in results]
    updated = jnp.concatenate(pieces, axis=1)
    return (unfold_rows(speed), unfold_rows(updated))


def solution(mesh):
    spec = P(("cases", "gx"), None, None)
    return jax.shard_map(
        per_device, mesh=mesh, in_specs=(spec, spec, spec), out_specs=(spec, spec), check_vma=False
    )
```

```python
import functools

import jax
import jax.numpy as jnp
from jax import lax
from jax.experimental import pallas as pl
from jax.experimental.pallas import tpu as pltpu
from jax.sharding import PartitionSpec as P

SWEEPS = 4
REINIT = 2
SUB = 8
SPLIT = (0, 4, 8)

weno_eps = 1e-06
advect_step = 0.15
reinit_step = 0.3


def recip(value):
    return pl.reciprocal(value, approx=True)


def face_pair(d, q6, s4, a, b, c, r_here, r_next):
    ratio_a = b * recip(a)
    ratio_c = b * recip(c)
    gain_a = ratio_a * ratio_a
    gain_c = ratio_c * ratio_c
    part_a = gain_a * r_here
    part_c = gain_c * r_next
    half = 0.5 * (gain_a + gain_c) + 3.0
    mid = d + 0.5 * q6
    minus = (mid + s4) - (part_a + 1.5 * part_c) * recip(half + gain_c)
    negated_plus = (s4 - mid) - (1.5 * part_a + part_c) * recip(half + gain_a)
    return minus, negated_plus


def smoothness(x, y, x_square, y_square):
    cross = x * y
    base = (x_square + y_square) + 0.75 * weno_eps
    outer = base - 2.75 * cross
    return outer + 1.5 * y_square, base - 1.25 * cross, outer + 1.5 * x_square


def along_line(cells):
    count = len(cells) - 6
    d = [cells[i + 1] - cells[i] for i in range(count + 5)]
    e = [d[i + 1] - d[i] for i in range(count + 4)]
    squares = [v * v for v in e]
    triples = [smoothness(e[i], e[i + 1], squares[i], squares[i + 1]) for i in range(count + 3)]
    q6 = [(e[i + 1] - e[i]) * (1.0 / 6.0) for i in range(count + 3)]
    r6 = [q6[i + 1] - q6[i] for i in range(count + 2)]
    faces = []
    for k in range(count + 1):
        s4 = 0.25 * (e[k + 1] + e[k + 2])
        faces.append(
            face_pair(
                d[k + 2], q6[k + 1], s4, triples[k][0], triples[k + 1][1], triples[k + 2][2], r6[k], r6[k + 1]
            )
        )
    return [(faces[i][0], faces[i + 1][1]) for i in range(count)]


def along_lanes(cell):
    length = cell.shape[1]
    cells = [cell if k == 0 else pltpu.roll(cell, -k % length, 1) for k in range(-2, 4)]
    d = [cells[i + 1] - cells[i] for i in range(5)]
    e = [d[i + 1] - d[i] for i in range(4)]
    squares = [v * v for v in e]
    a, b, c = [smoothness(e[i], e[i + 1], squares[i], squares[i + 1])[i] for i in range(3)]
    q6 = [(e[i + 1] - e[i]) * (1.0 / 6.0) for i in range(3)]
    s4 = 0.25 * (e[1] + e[2])
    minus, negated_plus = face_pair(d[2], q6[1], s4, a, b, c, q6[1] - q6[0], q6[2] - q6[1])
    return pltpu.roll(minus, 1, 1), negated_plus


def upwind(pair, positive):
    minus, negated_plus = pair
    rising = jnp.maximum(jnp.maximum(minus, negated_plus), 0.0)
    falling = jnp.minimum(jnp.minimum(minus, negated_plus), 0.0)
    chosen = jnp.where(positive, rising, falling)
    return chosen * chosen


def upwind_both(pair):
    minus, negated_plus = pair
    rising = jnp.maximum(jnp.maximum(minus, negated_plus), 0.0)
    falling = jnp.minimum(jnp.minimum(minus, negated_plus), 0.0)
    return rising * rising, falling * falling


def shift_rows(tile, down):
    rows = lax.broadcasted_iota(jnp.int32, tile.shape, 0)
    if down:
        return jnp.where(rows == 0, tile, pltpu.roll(tile, 1, 0))
    return jnp.where(rows == SUB - 1, tile, pltpu.roll(tile, SUB - 1, 0))


def edge_tile(wrapped, nearest_row_tile, low):
    rows = lax.broadcasted_iota(jnp.int32, wrapped.shape, 0)
    if low:
        return jnp.where(rows == 0, nearest_row_tile, pltpu.roll(wrapped, 1, 0))
    return jnp.where(rows == SUB - 1, nearest_row_tile, pltpu.roll(wrapped, SUB - 1, 0))


def local_body(chunks, both, block, *refs):
    u_refs = refs[:chunks]
    if both:
        rise_ref, fall_ref, padded = refs[chunks:]
    else:
        vel_ref, out_ref, padded = refs[chunks:]
    tiles = padded.shape[0] - 6
    start = 3
    for ref in u_refs:
        padded[start : start + ref.shape[1]] = ref[0]
        start += ref.shape[1]
    first = padded[3]
    final = padded[tiles + 2]
    for step in range(3):
        padded[step] = edge_tile(padded[tiles + step], first, True)
        padded[tiles + 3 + step] = edge_tile(padded[3 + step], final, False)

    def loop(number, carry):
        start = number * block
        cells = [padded[start + i] for i in range(block + 6)]
        pairs = along_line(cells)
        for i in range(block):
            lanes = along_lanes(cells[i + 3])
            if both:
                rise_y, fall_y = upwind_both(pairs[i])
                rise_z, fall_z = upwind_both(lanes)
                rise_ref[0, start + i] = rise_y + rise_z
                fall_ref[0, start + i] = fall_y + fall_z
            else:
                positive = vel_ref[0, start + i] > 0.0
                out_ref[0, start + i] = upwind(pairs[i], positive) + upwind(lanes, positive)
        return carry

    lax.fori_loop(0, tiles // block, loop, 0)


def local_part(pieces, velocity, block=16):
    layers, _, _, lanes = pieces[0].shape
    tiles = sum(piece.shape[1] for piece in pieces)
    both = velocity is None
    whole = pl.BlockSpec((1, tiles, SUB, lanes), lambda i: (i, 0, 0, 0))
    shape = jax.ShapeDtypeStruct((layers, tiles, SUB, lanes), jnp.float32)
    cells = layers * tiles * SUB * lanes
    return pl.pallas_call(
        functools.partial(local_body, len(pieces), both, block),
        grid=(layers,),
        in_specs=[pl.BlockSpec((1,) + p.shape[1:], lambda i: (i, 0, 0, 0)) for p in pieces] + ([] if both else [whole]),
        out_specs=(whole, whole) if both else whole,
        out_shape=(shape, shape) if both else shape,
        scratch_shapes=[pltpu.VMEM((tiles + 6, SUB, lanes), jnp.float32)],
        compiler_params=pltpu.CompilerParams(vmem_limit_bytes=24 * 1024 * 1024),
        cost_estimate=pl.CostEstimate(flops=130 * cells, bytes_accessed=12 * cells, transcendentals=8 * cells),
        name="local_part",
    )(*pieces, *(() if both else (velocity,)))


def finish_body(kind, last, *refs):
    parity_ref, u_ref, far_ref, near_ref = refs[:4]
    rest = list(refs[4:])
    even = parity_ref[0] == 0
    layers, tiles = u_ref.shape[0], u_ref.shape[1]
    if kind == "first":
        rise_ref, fall_ref, vel_ref = rest[:3]
        rest = rest[3:]
    else:
        local_ref, vel_ref = rest[:2]
        rest = rest[2:]
        if kind in ("second", "third"):
            base_ref = rest.pop(0)
    out_ref = rest[0]

    def loop(t, carry):
        own = [u_ref[i, t] for i in range(layers)]
        far = [far_ref[i, t] for i in range(3)]
        near = [near_ref[i, t] for i in range(3)]
        cells = [jnp.where(even, a, b) for a, b in zip(far, near)] + own + [jnp.where(even, b, a) for a, b in zip(far, near)]
        made = []
        pairs = along_line(cells)
        for i in range(layers):
            vel = vel_ref[i, t]
            positive = vel > 0.0
            total = upwind(pairs[i], positive)
            if kind == "first":
                total = total + jnp.where(positive, rise_ref[i, t], fall_ref[i, t])
            else:
                total = total + local_ref[i, t]
            height = jnp.sqrt(total)
            if kind == "first":
                new = own[i] - advect_step * (vel * height)
            elif kind == "second":
                new = 0.75 * base_ref[i, t] + 0.25 * (own[i] - advect_step * (vel * height))
            elif kind == "third":
                new = base_ref[i, t] * (1.0 / 3.0) + (2.0 / 3.0) * (own[i] - advect_step * (vel * height))
            else:
                sign = vel * lax.rsqrt(vel * vel + 1.0)
                new = own[i] - reinit_step * (sign * (height - 1.0))
            out_ref[i, t] = new
            made.append(new)
        if not last:
            for i in range(3):
                rest[1][i, t] = jnp.where(even, made[i], made[layers - 3 + i])
                rest[2][i, t] = jnp.where(even, made[layers - 3 + i], made[i])
        return carry

    lax.fori_loop(0, tiles, loop, 0, unroll=4)


def finish_part(kind, last, start, parity, u, far, near, others, block=4):
    layers, per, _, lanes = u.shape
    block = min(block, per)
    shift = start // block
    own = pl.BlockSpec((layers, block, SUB, lanes), lambda i: (0, i, 0, 0))
    side = pl.BlockSpec((3, block, SUB, lanes), lambda i: (0, i, 0, 0))
    moved = pl.BlockSpec((layers, block, SUB, lanes), lambda i: (0, i + shift, 0, 0))
    shape = jax.ShapeDtypeStruct(u.shape, jnp.float32)
    side_shape = jax.ShapeDtypeStruct((3, per, SUB, lanes), jnp.float32)
    specs = [moved if other.shape[1] != per else own for other in others]
    cells = layers * per * SUB * lanes
    return pl.pallas_call(
        functools.partial(finish_body, kind, last),
        grid=(per // block,),
        in_specs=[pl.BlockSpec(memory_space=pltpu.SMEM), own, side, side] + specs,
        out_specs=own if last else (own, side, side),
        out_shape=shape if last else (shape, side_shape, side_shape),
        compiler_params=pltpu.CompilerParams(vmem_limit_bytes=24 * 1024 * 1024),
        cost_estimate=pl.CostEstimate(flops=80 * cells, bytes_accessed=32 * cells, transcendentals=6 * cells),
        name="finish_part",
    )(parity, u, far, near, *others)


def sweep_body(parity_ref, far_ref, mid_ref, near_ref, weight_ref, fixed_ref, far_out, mid_out, near_out, padded):
    layers, tiles, lanes = weight_ref.shape[0], weight_ref.shape[1], weight_ref.shape[3]
    even = parity_ref[0] == 0
    padded[jnp.where(even, 0, layers - 1), 1 : tiles + 1] = far_ref[0]
    padded[jnp.where(even, layers - 1, 0), 1 : tiles + 1] = near_ref[0]
    for i in range(1, layers - 1):
        padded[i, 1 : tiles + 1] = mid_ref[i - 1]
    for i in range(layers):
        first, final = padded[i, 1], padded[i, tiles]
        padded[i, 0] = edge_tile(final, first, True)
        padded[i, tiles + 1] = edge_tile(first, final, False)

    def loop(t, carry):
        cells = [padded[i, t + 1] for i in range(layers)]
        ends = []
        for i in range(layers):
            total = padded[i, t] + padded[i, t + 2]
            total = total + pltpu.roll(cells[i], lanes - 1, 1) + pltpu.roll(cells[i], 1, 1)
            if i > 0:
                total = total + cells[i - 1]
            if i < layers - 1:
                total = total + cells[i + 1]
            weight = weight_ref[i, t]
            new = weight * fixed_ref[i, t] + (1.0 - weight) * (total * (1.0 / 6.0))
            if 0 < i < layers - 1:
                mid_out[i - 1, t] = new
            else:
                ends.append(new)
        far_out[0, t] = jnp.where(even, ends[0], ends[1])
        near_out[0, t] = jnp.where(even, ends[1], ends[0])
        return carry

    lax.fori_loop(0, tiles, loop, 0, unroll=16)


def sweep_part(parity, far, mid, near, weight, fixed):
    cells = weight.size
    layers, tiles, _, lanes = weight.shape
    vmem = pl.BlockSpec(memory_space=pltpu.VMEM)
    return pl.pallas_call(
        sweep_body,
        in_specs=[pl.BlockSpec(memory_space=pltpu.SMEM)] + [vmem] * 5,
        out_specs=(vmem, vmem, vmem),
        out_shape=tuple(jax.ShapeDtypeStruct(v.shape, jnp.float32) for v in (far, mid, near)),
        scratch_shapes=[pltpu.VMEM((layers, tiles + 2, SUB, lanes), jnp.float32)],
        compiler_params=pltpu.CompilerParams(vmem_limit_bytes=24 * 1024 * 1024),
        cost_estimate=pl.CostEstimate(flops=12 * cells, bytes_accessed=16 * cells, transcendentals=0),
        name="sweep_part",
    )(parity, far, mid, near, weight, fixed)


def fold_rows(array):
    layers, rows, lanes = array.shape
    return array.reshape(layers, SUB, rows // SUB, lanes).transpose(0, 2, 1, 3)


def unfold_rows(array):
    layers, tiles, _, lanes = array.shape
    return array.transpose(0, 2, 1, 3).reshape(layers, tiles * SUB, lanes)


def swap_far(array):
    count = lax.axis_size("gx")
    odd = range(1, count, 2)
    return lax.ppermute(array, "gx", [(i, (i + 1) % count) for i in odd] + [((i + 1) % count, i) for i in odd])


def swap_near(array):
    count = lax.axis_size("gx")
    return lax.ppermute(array, "gx", [(i, i + 1 - 2 * (i % 2)) for i in range(count)])


def per_device(level_set, sensitivity, band):
    layers = level_set.shape[0]
    weight = fold_rows(band).astype(jnp.float32)
    fixed = weight * fold_rows(sensitivity)
    level = fold_rows(level_set)
    bounds = [level.shape[1] * part // 8 for part in SPLIT]

    def cut(array):
        return [array[:, start:stop] for start, stop in zip(bounds, bounds[1:])]

    pieces = cut(level)
    parity = lax.rem(lax.axis_index("gx"), 2)
    even = parity == 0
    parity = parity.astype(jnp.int32).reshape(1)

    def order(first, second):
        return jnp.where(even, first, second), jnp.where(even, second, first)

    sides = list(zip(*[cut(side) for side in order(level[:3], level[layers - 3 :])]))

    edges = [slice(0, 1), slice(layers - 1, layers)]
    far, near = order(*[fold_rows(band[e].astype(jnp.float32) * sensitivity[e]) for e in edges])
    far_open, near_open = order(*[(1.0 - fold_rows(band[e]).astype(jnp.float32)) * (1.0 / 6.0) for e in edges])
    mid = fixed[1 : layers - 1]
    halos = [(swap_far(side[0]), swap_near(side[1])) for side in sides]
    rise, fall = local_part([level], None)
    for sweep in range(SWEEPS):
        from_far, from_near = swap_far(far), swap_near(near)
        far_part, mid, near_part = sweep_part(parity, far, mid, near, weight, fixed)
        if sweep == 0:
            mid, rise, fall = lax.optimization_barrier((mid, rise, fall))
        far = far_part + far_open * from_far
        near = near_part + near_open * from_near
    low, high = order(far, near)
    speed = jnp.concatenate([low, mid, high], axis=0)

    kinds = ["first", "second", "third"] + ["reinit"] * REINIT
    base = level
    marker = None
    for number, kind in enumerate(kinds):
        last = number == len(kinds) - 1
        if number > 0:
            halos = [(swap_far(far), swap_near(near)) for far, near in sides]
            if kind == "reinit" and marker is None:
                marker = pieces
            if kind == "reinit":
                local = local_part(pieces, jnp.concatenate(marker, axis=1))
            else:
                local = local_part(pieces, speed)
        results = []
        if last:
            updated = jnp.zeros((layers, SUB) + level.shape[1:2] + level.shape[3:], jnp.float32)
        for i in range(len(pieces)):
            if last and i > 0:
                updated, pieces[i] = lax.optimization_barrier((updated, pieces[i]))
            if kind == "first":
                others = (rise, fall, speed)
            elif kind == "reinit":
                others = (local, marker[i])
            else:
                others = (local, speed, level)
            result = finish_part(kind, last, bounds[i], parity, pieces[i], halos[i][0], halos[i][1], others)
            if last:
                updated = updated.at[:, :, bounds[i] : bounds[i + 1]].set(result.transpose(0, 2, 1, 3))
            results.append(result)
        if not last:
            pieces = [r[0] for r in results]
            sides = [r[1:] for r in results]
    return (unfold_rows(speed), updated.reshape(level_set.shape))


def solution(mesh):
    spec = P(("cases", "gx"), None, None)
    return jax.shard_map(
        per_device, mesh=mesh, in_specs=(spec, spec, spec), out_specs=(spec, spec), check_vma=False
    )
```

```python
import functools

import jax
import jax.numpy as jnp
from jax import lax
from jax.experimental import pallas as pl
from jax.experimental.pallas import tpu as pltpu
from jax.sharding import PartitionSpec as P

SWEEPS = 4
REINIT = 2
SUB = 8
SPLIT = (0, 4, 8)

weno_eps = 1e-06
advect_step = 0.15
reinit_step = 0.3


def recip(value):
    return pl.reciprocal(value, approx=True)


def face_pair(d, q6, s4, a, b, c, r_here, r_next):
    ratio_a = b * recip(a)
    ratio_c = b * recip(c)
    gain_a = ratio_a * ratio_a
    gain_c = ratio_c * ratio_c
    part_a = gain_a * r_here
    part_c = gain_c * r_next
    half = 0.5 * (gain_a + gain_c) + 3.0
    mid = d + 0.5 * q6
    minus = (mid + s4) - (part_a + 1.5 * part_c) * recip(half + gain_c)
    negated_plus = (s4 - mid) - (1.5 * part_a + part_c) * recip(half + gain_a)
    return minus, negated_plus


def smoothness(x, y, x_square, y_square):
    cross = x * y
    base = (x_square + y_square) + 0.75 * weno_eps
    outer = base - 2.75 * cross
    return outer + 1.5 * y_square, base - 1.25 * cross, outer + 1.5 * x_square


def along_line(cells):
    count = len(cells) - 6
    d = [cells[i + 1] - cells[i] for i in range(count + 5)]
    e = [d[i + 1] - d[i] for i in range(count + 4)]
    squares = [v * v for v in e]
    triples = [smoothness(e[i], e[i + 1], squares[i], squares[i + 1]) for i in range(count + 3)]
    q6 = [(e[i + 1] - e[i]) * (1.0 / 6.0) for i in range(count + 3)]
    r6 = [q6[i + 1] - q6[i] for i in range(count + 2)]
    faces = []
    for k in range(count + 1):
        s4 = 0.25 * (e[k + 1] + e[k + 2])
        faces.append(
            face_pair(
                d[k + 2], q6[k + 1], s4, triples[k][0], triples[k + 1][1], triples[k + 2][2], r6[k], r6[k + 1]
            )
        )
    return [(faces[i][0], faces[i + 1][1]) for i in range(count)]


def along_lanes(cell):
    length = cell.shape[1]
    cells = [cell if k == 0 else pltpu.roll(cell, -k % length, 1) for k in range(-2, 4)]
    d = [cells[i + 1] - cells[i] for i in range(5)]
    e = [d[i + 1] - d[i] for i in range(4)]
    squares = [v * v for v in e]
    a, b, c = [smoothness(e[i], e[i + 1], squares[i], squares[i + 1])[i] for i in range(3)]
    q6 = [(e[i + 1] - e[i]) * (1.0 / 6.0) for i in range(3)]
    s4 = 0.25 * (e[1] + e[2])
    minus, negated_plus = face_pair(d[2], q6[1], s4, a, b, c, q6[1] - q6[0], q6[2] - q6[1])
    return pltpu.roll(minus, 1, 1), negated_plus


def upwind(pair, positive):
    minus, negated_plus = pair
    rising = jnp.maximum(jnp.maximum(minus, negated_plus), 0.0)
    falling = jnp.minimum(jnp.minimum(minus, negated_plus), 0.0)
    chosen = jnp.where(positive, rising, falling)
    return chosen * chosen


def upwind_both(pair):
    minus, negated_plus = pair
    rising = jnp.maximum(jnp.maximum(minus, negated_plus), 0.0)
    falling = jnp.minimum(jnp.minimum(minus, negated_plus), 0.0)
    return rising * rising, falling * falling


def shift_rows(tile, down):
    rows = lax.broadcasted_iota(jnp.int32, tile.shape, 0)
    if down:
        return jnp.where(rows == 0, tile, pltpu.roll(tile, 1, 0))
    return jnp.where(rows == SUB - 1, tile, pltpu.roll(tile, SUB - 1, 0))


def edge_tile(wrapped, nearest_row_tile, low):
    rows = lax.broadcasted_iota(jnp.int32, wrapped.shape, 0)
    if low:
        return jnp.where(rows == 0, nearest_row_tile, pltpu.roll(wrapped, 1, 0))
    return jnp.where(rows == SUB - 1, nearest_row_tile, pltpu.roll(wrapped, SUB - 1, 0))


def local_body(chunks, both, block, *refs):
    u_refs = refs[:chunks]
    if both:
        rise_ref, fall_ref, padded = refs[chunks:]
    else:
        vel_ref, out_ref, padded = refs[chunks:]
    tiles = padded.shape[0] - 6
    start = 3
    for ref in u_refs:
        padded[start : start + ref.shape[1]] = ref[0]
        start += ref.shape[1]
    first = padded[3]
    final = padded[tiles + 2]
    for step in range(3):
        padded[step] = edge_tile(padded[tiles + step], first, True)
        padded[tiles + 3 + step] = edge_tile(padded[3 + step], final, False)

    def loop(number, carry):
        start = number * block
        cells = [padded[start + i] for i in range(block + 6)]
        pairs = along_line(cells)
        for i in range(block):
            lanes = along_lanes(cells[i + 3])
            if both:
                rise_y, fall_y = upwind_both(pairs[i])
                rise_z, fall_z = upwind_both(lanes)
                rise_ref[0, start + i] = rise_y + rise_z
                fall_ref[0, start + i] = fall_y + fall_z
            else:
                positive = vel_ref[0, start + i] > 0.0
                out_ref[0, start + i] = upwind(pairs[i], positive) + upwind(lanes, positive)
        return carry

    lax.fori_loop(0, tiles // block, loop, 0)


def local_part(pieces, velocity, block=16):
    layers, _, _, lanes = pieces[0].shape
    tiles = sum(piece.shape[1] for piece in pieces)
    both = velocity is None
    whole = pl.BlockSpec((1, tiles, SUB, lanes), lambda i: (i, 0, 0, 0))
    shape = jax.ShapeDtypeStruct((layers, tiles, SUB, lanes), jnp.float32)
    cells = layers * tiles * SUB * lanes
    return pl.pallas_call(
        functools.partial(local_body, len(pieces), both, block),
        grid=(layers,),
        in_specs=[pl.BlockSpec((1,) + p.shape[1:], lambda i: (i, 0, 0, 0)) for p in pieces] + ([] if both else [whole]),
        out_specs=(whole, whole) if both else whole,
        out_shape=(shape, shape) if both else shape,
        scratch_shapes=[pltpu.VMEM((tiles + 6, SUB, lanes), jnp.float32)],
        compiler_params=pltpu.CompilerParams(vmem_limit_bytes=24 * 1024 * 1024),
        cost_estimate=pl.CostEstimate(flops=130 * cells, bytes_accessed=12 * cells, transcendentals=8 * cells),
        name="local_part",
    )(*pieces, *(() if both else (velocity,)))


def finish_body(kind, last, *refs):
    parity_ref, u_ref, far_ref, near_ref = refs[:4]
    rest = list(refs[4:])
    even = parity_ref[0] == 0
    layers, tiles = u_ref.shape[0], u_ref.shape[1]
    if kind == "first":
        rise_ref, fall_ref, vel_ref = rest[:3]
        rest = rest[3:]
    else:
        local_ref, vel_ref = rest[:2]
        rest = rest[2:]
        if kind in ("second", "third"):
            base_ref = rest.pop(0)
    out_ref = rest[0]

    def loop(t, carry):
        own = [u_ref[i, t] for i in range(layers)]
        far = [far_ref[i, t] for i in range(3)]
        near = [near_ref[i, t] for i in range(3)]
        cells = [jnp.where(even, a, b) for a, b in zip(far, near)] + own + [jnp.where(even, b, a) for a, b in zip(far, near)]
        made = []
        pairs = along_line(cells)
        for i in range(layers):
            vel = vel_ref[i, t]
            positive = vel > 0.0
            total = upwind(pairs[i], positive)
            if kind == "first":
                total = total + jnp.where(positive, rise_ref[i, t], fall_ref[i, t])
            else:
                total = total + local_ref[i, t]
            height = jnp.sqrt(total)
            if kind == "first":
                new = own[i] - advect_step * (vel * height)
            elif kind == "second":
                new = 0.75 * base_ref[i, t] + 0.25 * (own[i] - advect_step * (vel * height))
            elif kind == "third":
                new = base_ref[i, t] * (1.0 / 3.0) + (2.0 / 3.0) * (own[i] - advect_step * (vel * height))
            else:
                sign = vel * lax.rsqrt(vel * vel + 1.0)
                new = own[i] - reinit_step * (sign * (height - 1.0))
            out_ref[i, t] = new
            made.append(new)
        if not last:
            for i in range(3):
                rest[1][i, t] = jnp.where(even, made[i], made[layers - 3 + i])
                rest[2][i, t] = jnp.where(even, made[layers - 3 + i], made[i])
        return carry

    lax.fori_loop(0, tiles, loop, 0, unroll=4)


def finish_part(kind, last, start, parity, u, far, near, others, block=4):
    layers, per, _, lanes = u.shape
    block = min(block, per)
    shift = start // block
    own = pl.BlockSpec((layers, block, SUB, lanes), lambda i: (0, i, 0, 0))
    side = pl.BlockSpec((3, block, SUB, lanes), lambda i: (0, i, 0, 0))
    moved = pl.BlockSpec((layers, block, SUB, lanes), lambda i: (0, i + shift, 0, 0))
    shape = jax.ShapeDtypeStruct(u.shape, jnp.float32)
    side_shape = jax.ShapeDtypeStruct((3, per, SUB, lanes), jnp.float32)
    specs = [moved if other.shape[1] != per else own for other in others]
    cells = layers * per * SUB * lanes
    return pl.pallas_call(
        functools.partial(finish_body, kind, last),
        grid=(per // block,),
        in_specs=[pl.BlockSpec(memory_space=pltpu.SMEM), own, side, side] + specs,
        out_specs=own if last else (own, side, side),
        out_shape=shape if last else (shape, side_shape, side_shape),
        compiler_params=pltpu.CompilerParams(vmem_limit_bytes=24 * 1024 * 1024),
        cost_estimate=pl.CostEstimate(flops=80 * cells, bytes_accessed=32 * cells, transcendentals=6 * cells),
        name="finish_part",
    )(parity, u, far, near, *others)


def sweep_body(parity_ref, far_ref, mid_ref, near_ref, weight_ref, fixed_ref, far_out, mid_out, near_out, padded):
    layers, tiles, lanes = weight_ref.shape[0], weight_ref.shape[1], weight_ref.shape[3]
    even = parity_ref[0] == 0
    padded[jnp.where(even, 0, layers - 1), 1 : tiles + 1] = far_ref[0]
    padded[jnp.where(even, layers - 1, 0), 1 : tiles + 1] = near_ref[0]
    for i in range(1, layers - 1):
        padded[i, 1 : tiles + 1] = mid_ref[i - 1]
    for i in range(layers):
        first, final = padded[i, 1], padded[i, tiles]
        padded[i, 0] = edge_tile(final, first, True)
        padded[i, tiles + 1] = edge_tile(first, final, False)

    def loop(t, carry):
        cells = [padded[i, t + 1] for i in range(layers)]
        ends = []
        for i in range(layers):
            total = padded[i, t] + padded[i, t + 2]
            total = total + pltpu.roll(cells[i], lanes - 1, 1) + pltpu.roll(cells[i], 1, 1)
            if i > 0:
                total = total + cells[i - 1]
            if i < layers - 1:
                total = total + cells[i + 1]
            weight = weight_ref[i, t]
            new = weight * fixed_ref[i, t] + (1.0 - weight) * (total * (1.0 / 6.0))
            if 0 < i < layers - 1:
                mid_out[i - 1, t] = new
            else:
                ends.append(new)
        far_out[0, t] = jnp.where(even, ends[0], ends[1])
        near_out[0, t] = jnp.where(even, ends[1], ends[0])
        return carry

    lax.fori_loop(0, tiles, loop, 0, unroll=16)


def sweep_part(parity, far, mid, near, weight, fixed):
    cells = weight.size
    layers, tiles, _, lanes = weight.shape
    vmem = pl.BlockSpec(memory_space=pltpu.VMEM)
    return pl.pallas_call(
        sweep_body,
        in_specs=[pl.BlockSpec(memory_space=pltpu.SMEM)] + [vmem] * 5,
        out_specs=(vmem, vmem, vmem),
        out_shape=tuple(jax.ShapeDtypeStruct(v.shape, jnp.float32) for v in (far, mid, near)),
        scratch_shapes=[pltpu.VMEM((layers, tiles + 2, SUB, lanes), jnp.float32)],
        compiler_params=pltpu.CompilerParams(vmem_limit_bytes=24 * 1024 * 1024),
        cost_estimate=pl.CostEstimate(flops=12 * cells, bytes_accessed=16 * cells, transcendentals=0),
        name="sweep_part",
    )(parity, far, mid, near, weight, fixed)


def fold_rows(array):
    layers, rows, lanes = array.shape
    return array.reshape(layers, SUB, rows // SUB, lanes).transpose(0, 2, 1, 3)


def unfold_rows(array):
    layers, tiles, _, lanes = array.shape
    return array.transpose(0, 2, 1, 3).reshape(layers, tiles * SUB, lanes)


def swap_far(array):
    count = lax.axis_size("gx")
    odd = range(1, count, 2)
    return lax.ppermute(array, "gx", [(i, (i + 1) % count) for i in odd] + [((i + 1) % count, i) for i in odd])


def swap_near(array):
    count = lax.axis_size("gx")
    return lax.ppermute(array, "gx", [(i, i + 1 - 2 * (i % 2)) for i in range(count)])


def per_device(level_set, sensitivity, band):
    layers = level_set.shape[0]
    weight = fold_rows(band).astype(jnp.float32)
    fixed = weight * fold_rows(sensitivity)
    level = fold_rows(level_set)
    bounds = [level.shape[1] * part // 8 for part in SPLIT]

    def cut(array):
        return [array[:, start:stop] for start, stop in zip(bounds, bounds[1:])]

    pieces = cut(level)
    parity = lax.rem(lax.axis_index("gx"), 2)
    even = parity == 0
    parity = parity.astype(jnp.int32).reshape(1)

    def order(first, second):
        return jnp.where(even, first, second), jnp.where(even, second, first)

    sides = list(zip(*[cut(side) for side in order(level[:3], level[layers - 3 :])]))

    edges = [slice(0, 1), slice(layers - 1, layers)]
    far, near = order(*[fold_rows(band[e].astype(jnp.float32) * sensitivity[e]) for e in edges])
    far_open, near_open = order(*[(1.0 - fold_rows(band[e]).astype(jnp.float32)) * (1.0 / 6.0) for e in edges])
    mid = fixed[1 : layers - 1]
    halos = [(swap_far(side[0]), swap_near(side[1])) for side in sides]
    rise, fall = local_part([level], None)
    for sweep in range(SWEEPS):
        from_far, from_near = swap_far(far), swap_near(near)
        far_part, mid, near_part = sweep_part(parity, far, mid, near, weight, fixed)
        if sweep == 0:
            mid, rise, fall = lax.optimization_barrier((mid, rise, fall))
        far = far_part + far_open * from_far
        near = near_part + near_open * from_near
    low, high = order(far, near)
    speed = jnp.concatenate([low, mid, high], axis=0)

    kinds = ["first", "second", "third"] + ["reinit"] * REINIT
    base = level
    marker = None
    for number, kind in enumerate(kinds):
        last = number == len(kinds) - 1
        if number > 0:
            from_near = [swap_near(near) for far, near in sides]
            halos = list(zip([swap_far(far) for far, near in sides], from_near))
            if kind == "reinit" and marker is None:
                marker = pieces
            if kind == "reinit":
                local = local_part(pieces, jnp.concatenate(marker, axis=1))
            else:
                local = local_part(pieces, speed)
        results = []
        if last:
            updated = jnp.zeros((layers, SUB) + level.shape[1:2] + level.shape[3:], jnp.float32)
        for i in range(len(pieces)):
            if last and i > 0:
                updated, pieces[i] = lax.optimization_barrier((updated, pieces[i]))
            if kind == "first":
                others = (rise, fall, speed)
            elif kind == "reinit":
                others = (local, marker[i])
            else:
                others = (local, speed, level)
            result = finish_part(kind, last, bounds[i], parity, pieces[i], halos[i][0], halos[i][1], others)
            if last:
                updated = updated.at[:, :, bounds[i] : bounds[i + 1]].set(result.transpose(0, 2, 1, 3))
            results.append(result)
        if not last:
            pieces = [r[0] for r in results]
            sides = [r[1:] for r in results]
    return (unfold_rows(speed), updated.reshape(level_set.shape))


def solution(mesh):
    spec = P(("cases", "gx"), None, None)
    return jax.shard_map(
        per_device, mesh=mesh, in_specs=(spec, spec, spec), out_specs=(spec, spec), check_vma=False
    )
```
